32 devices in a mesh: tile: 4 (over x, core), bulk: 8 (over z, y).
Axes of the slice: x: 2, y: 2, z: 4, core: 2. Of those that a mesh axis runs over, the one named last changes fastest.
Arguments:
- coarse_now: float32 [256, 512, 128], P('tile', 'bulk'), may hold values from -6 to 6
- coarse_before: float32 [256, 512, 128], P('tile', 'bulk'), may hold values from -6 to 6
- coarse_courant: float32 [256, 512, 128], P('tile', 'bulk'), may hold values from 0.05 to 0.3
- coarse_absorb: float32 [256, 512, 128], P('tile', 'bulk'), may hold values from 0.02 to 0.3
- fine_now: float32 [64, 48, 2304], P(('tile', 'bulk')), may hold values from -6 to 6
- fine_before: float32 [64, 48, 2304], P(('tile', 'bulk')), may hold values from -6 to 6
- fine_courant: float32 [64, 48, 2304], P(('tile', 'bulk')), may hold values from 0.05 to 0.3
- fine_absorb: float32 [64, 48, 2304], P(('tile', 'bulk')), may hold values from 0.02 to 0.3
- box_anchor: int32 [64, 3], P(('tile', 'bulk')), may hold values from 0 to 496, as said below
- intersection: int32 [32, 4, 4], P(('tile', 'bulk')), may hold values from -1 to 112, as said below
Outputs:
- coarse_next: float32 [256, 512, 128], P('tile', 'bulk')
- coarse_last: float32 [256, 512, 128], P('tile', 'bulk')
- fine_next: float32 [64, 48, 2304], P(('tile', 'bulk'))
- fine_last: float32 [64, 48, 2304], P(('tile', 'bulk'))
The draws below stay inside these ranges and needn't reach their ends.
Inputs may be any that keep to these rules, and one draw needn't show every extreme that they name: `box_anchor`: box b is held in the box order of the fine arrays, by device d = b // 2; its region of 16 coarse cells along each dimension from its anchor lies inside the coarse block of device d, d XOR 1, d XOR h or d XOR h XOR 1, where h is half the number of devices; anchors are multiples of 16, and no two regions share a cell. `intersection`: row 0 lists each box exactly once, in the block of the device whose coarse cells hold its region, -1 in unused entries; rows 1 to 3 give that region's first cell relative to the block (0 in unused entries), matching box_anchor. Some block holds exactly 4 boxes.
All inputs are finite; a program needn't handle non-finite values.
Results may differ from the reference program's by a relative error of at most 0.0001.
Values sent between devices are 32-bit elements; how exact they have to be, the bound alone decides.
A program may use at most 512 MiB of HBM per device.

```python
import math
import jax
import jax.numpy as jnp
from jax import lax

CX = 64
CY = 64
NZ = 128
BC = 16
FINE = 48
BOX_DEV = 2
MOST = 4
STEPS = 2
BOXES = 64
NX = 256
NY = 512
N_BULK = 8
DEVICES = 32


def layout(key):
    half = DEVICES // 2
    quads = DEVICES // 4
    along_y = CY // BC
    along_z = NZ // BC
    places = CX // BC * along_y * along_z
    first, second, third = jax.random.split(key, 3)
    crowded = jax.random.randint(first, (), 0, quads)
    mirrored = (crowded + 1) % quads
    numbers = jnp.arange(BOXES, dtype=jnp.int32)
    holder = numbers // BOX_DEV
    quad = holder % half // 2
    local = holder % 2 + 2 * (holder // half)
    member = local * BOX_DEV + numbers % BOX_DEV
    orders = jax.vmap(lambda k: jax.random.permutation(k, 4 * MOST))(jax.random.split(second, quads)).astype(jnp.int32)
    picked = orders[quad, member]
    chosen_local = picked // MOST
    chosen_within = picked % MOST
    crowd_local = jnp.where(local % 2 == 0, 1, 0)
    crowd_within = local // 2 * BOX_DEV + numbers % BOX_DEV
    mirror_local = jnp.bitwise_xor(local, 2)
    mirror_within = numbers % BOX_DEV
    target_local = jnp.where(quad == crowded, crowd_local, jnp.where(quad == mirrored, mirror_local, chosen_local))
    within = jnp.where(quad == crowded, crowd_within, jnp.where(quad == mirrored, mirror_within, chosen_within)).astype(jnp.int32)
    block = (2 * quad + target_local % 2 + half * (target_local // 2)).astype(jnp.int32)
    box_slot = (block * MOST + within).astype(jnp.int32)
    rotate = jax.random.randint(third, (DEVICES,), 0, places)
    position = (within + rotate[block]) % places
    offsets = jnp.stack([position // (along_y * along_z) * BC, position // along_z % along_y * BC, position % along_z * BC])
    return (box_slot, block, offsets.astype(jnp.int32))


def draw_box_anchor(key, part):
    box_slot, block, offsets = layout(key)
    first_dim = block // N_BULK * CX + offsets[0]
    second_dim = block % N_BULK * CY + offsets[1]
    return jnp.stack([first_dim, second_dim, offsets[2]], axis=1).astype(jnp.int32)


def draw_intersection(key, part):
    box_slot, block, offsets = layout(key)
    total = DEVICES * MOST
    idents = jnp.full((total,), -1, jnp.int32).at[box_slot].set(jnp.arange(BOXES, dtype=jnp.int32))
    starts = jnp.zeros((3, total), jnp.int32).at[:, box_slot].set(offsets)
    table = jnp.concatenate([idents[None], starts], axis=0)
    return jnp.transpose(table.reshape(4, DEVICES, MOST), (1, 0, 2)).astype(jnp.int32)


def block_levels(own_key, extent, pieces, least, high):
    def one(axis_at, shards_of):
        draws = jax.random.uniform(jax.random.fold_in(jax.random.fold_in(own_key, 6), axis_at), (shards_of,), jnp.float32, least / len(pieces), high / len(pieces))
        return jnp.repeat(jnp.exp(draws), extent[axis_at] // shards_of).reshape((-1,) + (1,) * (len(extent) - axis_at - 1))

    factor_of = one(*pieces[0])
    for cut in pieces[1:]:
        factor_of = factor_of * one(*cut)
    return factor_of


def centred(own_key, dims, spread, bound, shards=(), kind=jnp.bfloat16):
    gain = block_levels(own_key, dims, shards, -0.22, 0.18) if shards else 1.0
    values = jax.random.normal(own_key, dims, jnp.float32) * spread * gain
    return jnp.minimum(jnp.maximum(values, -bound), bound).astype(kind)


def setup_inputs(seed: int = 0) -> dict:
    arg_keys = jax.random.split(jax.random.key(seed), 11)
    return {
        "coarse_now": centred(arg_keys[0], (NX, NY, NZ), 1.0, 6.0, ((0, 4), (1, 8)), jnp.float32),
        "coarse_before": centred(arg_keys[1], (NX, NY, NZ), 1.0, 6.0, ((0, 4), (1, 8)), jnp.float32),
        "coarse_courant": jnp.clip(jnp.exp(math.log(0.3) - 1.7917595 * jax.random.uniform(arg_keys[2], (NX, NY, NZ), jnp.float32) ** block_levels(arg_keys[2], (NX, NY, NZ), ((0, 4), (1, 8)), -0.2, 0.2)), 0.05, 0.3),
        "coarse_absorb": jnp.clip(jnp.exp(math.log(0.3) - 2.7080503 * jax.random.uniform(arg_keys[3], (NX, NY, NZ), jnp.float32) ** block_levels(arg_keys[3], (NX, NY, NZ), ((0, 4), (1, 8)), -0.2, 0.2)), 0.02, 0.3),
        "fine_now": centred(arg_keys[4], (BOXES, FINE, FINE * FINE), 1.0, 6.0, ((0, 32),), jnp.float32),
        "fine_before": centred(arg_keys[5], (BOXES, FINE, FINE * FINE), 1.0, 6.0, ((0, 32),), jnp.float32),
        "fine_courant": jnp.clip(jnp.exp(math.log(0.3) - 1.7917595 * jax.random.uniform(arg_keys[6], (BOXES, FINE, FINE * FINE), jnp.float32) ** block_levels(arg_keys[6], (BOXES, FINE, FINE * FINE), ((0, 32),), -0.2, 0.2)), 0.05, 0.3),
        "fine_absorb": jnp.clip(jnp.exp(math.log(0.3) - 2.7080503 * jax.random.uniform(arg_keys[7], (BOXES, FINE, FINE * FINE), jnp.float32) ** block_levels(arg_keys[7], (BOXES, FINE, FINE * FINE), ((0, 32),), -0.2, 0.2)), 0.02, 0.3),
        "box_anchor": draw_box_anchor(jax.random.fold_in(arg_keys[10], 71), 0),
        "intersection": draw_intersection(jax.random.fold_in(arg_keys[10], 71), 0),
    }


def fine_update(field, before, courant, absorb, ghosts):
    xm = jnp.concatenate([ghosts[0][None], field[:-1]], 0)
    xp = jnp.concatenate([field[1:], ghosts[1][None]], 0)
    ym = jnp.concatenate([ghosts[2][:, None, :], field[:, :-1]], 1)
    yp = jnp.concatenate([field[:, 1:], ghosts[3][:, None, :]], 1)
    zm = jnp.concatenate([ghosts[4][:, :, None], field[:, :, :-1]], 2)
    zp = jnp.concatenate([field[:, :, 1:], ghosts[5][:, :, None]], 2)
    lap = xm + xp + ym + yp + zm + zp - 6.0 * field
    return (2.0 * field - (1.0 - absorb) * before + courant * lap) / (1.0 + absorb)


def upsample(faces):
    return jnp.repeat(jnp.repeat(faces, 3, axis=-2), 3, axis=-1)


def coarse_update(padded, now, before, courant, absorb):
    centre = padded[1:-1, 1:-1, 1:-1]
    beside = padded[2:, 1:-1, 1:-1] + padded[:-2, 1:-1, 1:-1]
    beside = beside + padded[1:-1, 2:, 1:-1] + padded[1:-1, :-2, 1:-1]
    beside = beside + padded[1:-1, 1:-1, 2:] + padded[1:-1, 1:-1, :-2]
    lap = beside - 6.0 * centre
    return (2.0 * now - (1.0 - absorb) * before + courant * lap) / (1.0 + absorb)


def box_faces(padded, start, edge):
    cube = lax.dynamic_slice(padded, (start[0], start[1], start[2]), (edge + 2, edge + 2, edge + 2))
    inner = slice(1, edge + 1)
    return jnp.stack([cube[0, inner, inner], cube[edge + 1, inner, inner], cube[inner, 0, inner], cube[inner, edge + 1, inner], cube[inner, inner, 0], cube[inner, inner, edge + 1]])


def insert_blocks(field, restricted, intersection):
    entries = jnp.transpose(intersection, (0, 2, 1)).reshape(DEVICES * MOST, 4).astype(jnp.int32)
    owners = (jnp.arange(DEVICES * MOST) // MOST).astype(jnp.int32)

    def place_one(index, field):
        row = entries[index]
        device = owners[index]
        ident = row[0]
        safe = jnp.maximum(ident, 0)
        corner = (((device // N_BULK) * CX + row[1]).astype(jnp.int32), ((device % N_BULK) * CY + row[2]).astype(jnp.int32), row[3].astype(jnp.int32))
        current = lax.dynamic_slice(field, corner, (BC, BC, BC))
        block = jnp.where(ident >= 0, restricted[safe], current)
        return lax.dynamic_update_slice(field, block, corner)

    return lax.fori_loop(0, DEVICES * MOST, place_one, field)


def reference(coarse_now, coarse_before, coarse_courant, coarse_absorb, fine_now, fine_before, fine_courant, fine_absorb, box_anchor, intersection):
    shape = (BOXES, FINE, FINE, FINE)
    fine = fine_now.reshape(shape)
    fine_prev = fine_before.reshape(shape)
    fine_c = fine_courant.reshape(shape)
    fine_a = fine_absorb.reshape(shape)
    now = coarse_now
    before = coarse_before
    anchors = box_anchor.astype(jnp.int32)
    faces_all = jax.vmap(box_faces, (None, 0, None))
    for step in range(STEPS):
        padded = jnp.pad(now, 1)
        new = coarse_update(padded, now, before, coarse_courant, coarse_absorb)
        padded_new = jnp.pad(new, 1)
        old_faces = faces_all(padded, anchors, BC)
        new_faces = faces_all(padded_new, anchors, BC)
        for sub in range(3):
            weight = sub / 3.0
            ghosts = upsample(old_faces + weight * (new_faces - old_faces))
            ahead = jax.vmap(fine_update)(fine, fine_prev, fine_c, fine_a, ghosts)
            fine_prev = fine
            fine = ahead
        restricted = fine.reshape(BOXES, BC, 3, BC, 3, BC, 3).mean(axis=(2, 4, 6))
        new = insert_blocks(new, restricted, intersection)
        before = now
        now = new
    flat = (BOXES, FINE, FINE * FINE)
    return now, before, fine.reshape(flat), fine_prev.reshape(flat)
```

```python
import functools

import jax
import jax.numpy as jnp
import ml_dtypes
import numpy as np
from jax import lax
from jax.experimental import pallas as pl
from jax.experimental.pallas import tpu as pltpu
from jax.sharding import PartitionSpec as P

STEPS = 2
MESH = pl.DeviceIdType.MESH
BC, FINE = 16, 48
ROW = FINE * FINE
EDGE = 128
bf16 = jnp.bfloat16


def constants():
    flat = np.arange(ROW)
    y, z = flat // FINE, flat % FINE
    group = np.arange(BC)[:, None]
    spread = np.zeros((128, ROW), np.float32)
    spread[0:16] = (y == 0) & (z // 3 == group)
    spread[16:32] = (y == FINE - 1) & (z // 3 == group)
    spread[32:48] = (z == 0) & (y // 3 == group)
    spread[48:64] = (z == FINE - 1) & (y // 3 == group)
    spread[64:80] = z // 3 == group
    spread = np.concatenate([spread, spread], 0)
    up = np.zeros((160, 96), np.float32)
    for box in range(2):
        for x in range(FINE):
            up[box * 48 + x, box * 48 + x // 3] = 1
        for r in range(32):
            up[96 + box * 32 + r, box * 48 + 16 + r] = 1
    rows = (y // 3 == group).astype(np.float32)
    inside = np.stack([np.tile(z != 0, (8, 1)), np.tile(z != FINE - 1, (8, 1))]).astype(np.float32)
    down = np.zeros((16, 96), np.float32)
    for x in range(FINE):
        down[x // 3, x] = 1
        down[x // 3, 48 + x] = 1
    gather = np.zeros((ROW, 256), np.float32)
    gather[flat, (y // 3) * 16 + z // 3] = 1
    rep = np.zeros((256, 16), np.float32)
    rep[np.arange(256), np.arange(256) // 16] = 1
    own = (np.arange(256)[:, None] % 16 == np.arange(256)[None] // 16).astype(np.float32)
    tile = (np.arange(256)[:, None] % 16 == np.arange(128)[None] % 16).astype(np.float32)
    tile = np.concatenate([tile, tile], 0)
    half = ml_dtypes.bfloat16
    return [
        spread.astype(half), up.astype(half), rows, inside, down.astype(half),
        gather.astype(half), rep.astype(half), own, tile.astype(half),
    ]


def split(value):
    high = value.astype(bf16)
    low = (value - high.astype(jnp.float32)).astype(bf16)
    return high, low


def dot(a, b):
    return jnp.dot(a, b, preferred_element_type=jnp.float32)


def kernel(
    nt, nb,
    inter, anchor,
    now_h, before_h, courant_h, absorb_h, fnow_h, fbefore_h, fcourant_h, fabsorb_h,
    spread, up, rows, inside, down, gather, rep, own, tile,
    next_h, last_h, fnext_h, flast_h,
    p0, p1, p2, q0, rc, r2, fa, fb, frc, fr2,
    halo_out, halo_in, face_out, face_in, rest_out, rest_in,
    ghost, blocks, cubes, edges,
    halo_ss, halo_rs, face_ss, face_rs, rest_ss, rest_rs, load_sem, store_sem,
):
    t, b = lax.axis_index("tile"), lax.axis_index("bulk")
    fields = [p0, p1, p2]
    nx, ny = 64, 64

    exists = [t > 0, t < nt - 1, b > 0, b < nb - 1]
    missing = [t == 0, t == nt - 1, b == 0, b == nb - 1]
    beside = [(t - 1, b), (t + 1, b), (t, b - 1), (t, b + 1)]
    b_other = b + 1 - 2 * lax.rem(b, 2)
    t_other = lax.rem(t + nt // 2, nt)
    quad = [(t, b), (t, b_other), (t_other, b), (t_other, b_other)]

    mid = (pl.ds(1, nx), pl.ds(8, ny), slice(None))
    fmid = (slice(None), pl.ds(8, FINE), pl.ds(EDGE, ROW))
    loads = [
        pltpu.make_async_copy(src, dst, load_sem.at[i])
        for i, (src, dst) in enumerate([
            (now_h, p0.at[mid]),
            (before_h, q0),
            (courant_h, rc),
            (absorb_h, r2),
            (fnow_h, fa.at[fmid]),
            (fbefore_h, fb.at[fmid]),
            (fcourant_h, frc),
            (fabsorb_h, fr2),
        ])
    ]
    for load in loads:
        load.start()

    barrier = pltpu.get_barrier_semaphore()
    for have, device in zip(exists, beside):
        @pl.when(have)
        def _(device=device):
            pl.semaphore_signal(barrier, inc=1, device_id=device, device_id_type=MESH)
    for device in quad[2:]:
        pl.semaphore_signal(barrier, inc=1, device_id=device, device_id_type=MESH)
    peers = jnp.int32(2)
    for have in exists:
        peers = peers + jnp.where(have, 1, 0)
    pl.semaphore_wait(barrier, peers)

    zero_side = jnp.zeros((2, 64, EDGE), jnp.float32)
    for buf in (fa, fb):
        buf[:, :, pl.ds(0, EDGE)] = zero_side
        buf[:, :, pl.ds(EDGE + ROW, EDGE)] = zero_side

    lane = lax.broadcasted_iota(jnp.int32, (64, 128), 1)
    not_first, not_last = lane != 0, lane != 127

    def halo_wait(phase, side):
        return pltpu.make_async_remote_copy(
            src_ref=halo_out.at[phase, side],
            dst_ref=halo_in.at[phase, side],
            send_sem=halo_ss.at[phase, side],
            recv_sem=halo_rs.at[phase, side],
            device_id=beside[side],
            device_id_type=MESH,
        )

    def halo_copy(phase, side):
        return pltpu.make_async_remote_copy(
            src_ref=halo_out.at[phase, side],
            dst_ref=halo_in.at[phase, side ^ 1],
            send_sem=halo_ss.at[phase, side],
            recv_sem=halo_rs.at[phase, side ^ 1],
            device_id=beside[side],
            device_id_type=MESH,
        )

    def send_halo(phase, field):
        halo_out[phase, 0] = field[1, pl.ds(8, ny), :]
        halo_out[phase, 1] = field[nx, pl.ds(8, ny), :]
        halo_out[phase, 2] = field[pl.ds(1, nx), 8, :]
        halo_out[phase, 3] = field[pl.ds(1, nx), 7 + ny, :]
        for side in range(4):
            @pl.when(exists[side])
            def _(side=side):
                halo_copy(phase, side).start()

    def take_halo(phase, field):
        for side in range(4):
            @pl.when(exists[side])
            def _(side=side):
                halo_wait(phase, side).wait_recv()

            @pl.when(missing[side])
            def _(side=side):
                halo_in[phase, side] = jnp.zeros((64, 128), jnp.float32)
        field[0, pl.ds(8, ny), :] = halo_in[phase, 0]
        field[nx + 1, pl.ds(8, ny), :] = halo_in[phase, 1]
        field[pl.ds(1, nx), 7, :] = halo_in[phase, 2]
        field[pl.ds(1, nx), 8 + ny, :] = halo_in[phase, 3]

    def face_copy(phase, j):
        return pltpu.make_async_remote_copy(
            src_ref=face_out.at[phase, j - 1],
            dst_ref=face_in.at[phase, j],
            send_sem=face_ss.at[phase, j - 1],
            recv_sem=face_rs.at[phase, j - 1],
            device_id=quad[j],
            device_id_type=MESH,
        )

    def rest_copy(step, j):
        return pltpu.make_async_remote_copy(
            src_ref=rest_out.at[step],
            dst_ref=rest_in.at[step, j],
            send_sem=rest_ss.at[step, j - 1],
            recv_sem=rest_rs.at[step, j - 1],
            device_id=quad[j],
            device_id_type=MESH,
        )

    lane16 = lax.broadcasted_iota(jnp.int32, (16, 128), 1)
    z_in = lax.broadcasted_iota(jnp.int32, (256, 128), 0)
    z_in = lax.rem(z_in, 128)
    z_out = lax.broadcasted_iota(jnp.int32, (256, 128), 1)
    y_row = lax.broadcasted_iota(jnp.int32, (16, 16, 128), 1)
    y_lane = lax.rem(lax.broadcasted_iota(jnp.int32, (16, 16, 128), 2), 16)

    def collect(field):
        at = [4 * lax.div(inter[0, 1, e], 16) + lax.div(inter[0, 2, e], 16) for e in range(4)]
        spots = [jnp.full((16, 128), a, jnp.int32) for a in at]

        def choose(load, height, store):
            values = [None] * 4
            for i in range(4):
                for j in range(4):
                    value = load(i, j)
                    for e in range(4):
                        if i + j == 0:
                            values[e] = value
                        else:
                            values[e] = jnp.where(spots[e][:height] == 4 * i + j, value, values[e])
            for e in range(4):
                store(e, values[e])

        def to_edges(row, height):
            def store(e, value):
                edges[e, pl.ds(row, height), :] = value
            return store

        choose(lambda i, j: field[16 * i, pl.ds(8 + 16 * j, 16), :], 16, to_edges(32, 16))
        choose(lambda i, j: field[16 * i + 17, pl.ds(8 + 16 * j, 16), :], 16, to_edges(48, 16))

        @pl.loop(0, 16)
        def _(u):
            def to_cubes(e, value):
                cubes[e, pl.ds(pl.multiple_of(16 * u, 16), 16), :] = value
            choose(lambda i, j: field[16 * i + 1 + u, pl.ds(8 + 16 * j, 16), :], 16, to_cubes)
            choose(lambda i, j: field[16 * i + 1 + u, pl.ds(7 + 16 * j, 1), :], 1, to_edges(u, 1))
            choose(lambda i, j: field[16 * i + 1 + u, pl.ds(24 + 16 * j, 1), :], 1, to_edges(16 + u, 1))

    def faces_of(ref, entry):
        z0 = inter[0, 3, entry]
        high, low = split(cubes[entry])
        pick = ((z_in == z0 - 1) & (z_out >= 32) & (z_out < 48)) | (
            (z_in == z0 + 16) & (z_out >= 48) & (z_out < 64)
        )
        pick = jnp.where(pick, 1.0, 0.0).astype(bf16)
        zs = dot(jnp.concatenate([high, low], axis=1), pick).reshape(16, 16, 128)
        zs = jnp.sum(jnp.where(y_row == y_lane, zs, 0.0), axis=1)
        high, low = split(edges[entry])
        window = jnp.where(z_in == z0 + lax.rem(z_out, 16), 1.0, 0.0).astype(bf16)
        flat = dot(jnp.concatenate([high, low], axis=1), window)
        first = jnp.where(lane16 < 16, flat[0:16], jnp.where(lane16 < 32, flat[16:32], zs))
        x_lanes = (lane16 >= 64) & (lane16 < 80)
        ref[pl.ds(0, 16), :] = jnp.where(lane16 < 64, first, 0.0)
        ref[pl.ds(16, 16), :] = jnp.where(x_lanes, flat[32:48], 0.0)
        ref[pl.ds(32, 16), :] = jnp.where(x_lanes, flat[48:64], 0.0)

    def faces_for(j, slot):
        target = 2 * (quad[j][0] * nb + quad[j][1]) + slot
        value = blocks[0, pl.ds(0, 48), :]
        for entry in range(1, 4):
            hit = inter[0, 0, entry] == target
            value = jnp.where(hit, blocks[entry, pl.ds(0, 48), :], value)
        return value

    def send_faces(phase, field):
        collect(field)

        @pl.loop(0, 4)
        def _(entry):
            faces_of(blocks.at[entry, pl.ds(0, 48), :], entry)
        for j in range(1, 4):
            for slot in range(2):
                face_out[phase, j - 1, slot] = faces_for(j, slot)
            face_copy(phase, j).start()
        for slot in range(2):
            face_in[phase, 0, slot] = faces_for(0, slot)

    def take_faces(phase):
        for j in range(1, 4):
            face_copy(phase, j).wait_recv()

    def source_of(slot):
        away_t = jnp.where(lax.div(anchor[slot, 0], 64) == t, 0, 2)
        away_b = jnp.where(lax.div(anchor[slot, 1], 64) == b, 0, 1)
        return away_t + away_b

    sources = [source_of(slot) for slot in range(2)]

    def arrived(phase, slot):
        value = face_in[phase, 0, slot]
        for j in range(1, 4):
            value = jnp.where(sources[slot] == j, face_in[phase, j, slot], value)
        return value

    def coarse_update(new, field, before):
        @pl.loop(0, nx)
        def _(x):
            c = field[x + 1, pl.ds(8, ny), :]
            nbs = field[x, pl.ds(8, ny), :] + field[x + 2, pl.ds(8, ny), :]
            nbs = nbs + field[x + 1, pl.ds(7, ny), :] + field[x + 1, pl.ds(9, ny), :]
            nbs = nbs + jnp.where(not_first, pltpu.roll(c, 1, 1), 0.0)
            nbs = nbs + jnp.where(not_last, pltpu.roll(c, 127, 1), 0.0)
            old = before(x)
            new[x + 1, pl.ds(8, ny), :] = old + r2[x] * (c - old) + rc[x] * (nbs - 6.0 * c)

    row = lax.broadcasted_iota(jnp.int32, (8, ROW), 0)

    def make_ghosts(f, phase, weight):
        parts = []
        for slot in range(2):
            q = arrived(2 * phase, slot)
            if weight:
                q = q + weight * (arrived(2 * phase + 1, slot) - q)
            parts.append(q)
        high, low = split(jnp.concatenate(parts, axis=0))
        left = dot(up[...], jnp.concatenate([high, low], axis=1)).astype(bf16)

        @pl.loop(0, 9)
        def _(c):
            cols = pl.ds(pl.multiple_of(c * 256, 256), 256)
            ghost[:, cols] = dot(left, spread[:, cols])
        for slot in range(2):
            for k in range(2):
                face = ghost[pl.ds(96 + 32 * slot + 16 * k, 16), :] * rows[...]
                f[slot, pl.ds(7 + 49 * k, 1), pl.ds(EDGE, ROW)] = jnp.sum(face, axis=0, keepdims=True)

    def fine_update(f, g, slot):
        @pl.loop(0, 6)
        def _(i):
            base = pl.multiple_of(8 * i, 8)
            prev = f[slot, pl.ds(base, 8), pl.ds(EDGE, ROW)]
            after = f[slot, pl.ds(pl.multiple_of(base + 16, 8), 8), pl.ds(EDGE, ROW)]
            wide = f[slot, pl.ds(pl.multiple_of(base + 8, 8), 8), :]
            c = wide[:, EDGE:EDGE + ROW]
            width = ROW + 2 * EDGE
            nbs = jnp.where(row == 0, pltpu.roll(prev, 1, 0), pltpu.roll(c, 1, 0))
            nbs = nbs + jnp.where(row == 7, pltpu.roll(after, 7, 0), pltpu.roll(c, 7, 0))
            nbs = nbs + pltpu.roll(wide, FINE, 1)[:, EDGE:EDGE + ROW]
            nbs = nbs + pltpu.roll(wide, width - FINE, 1)[:, EDGE:EDGE + ROW]
            nbs = nbs + pltpu.roll(wide, 1, 1)[:, EDGE:EDGE + ROW] * inside[0]
            nbs = nbs + pltpu.roll(wide, width - 1, 1)[:, EDGE:EDGE + ROW] * inside[1]
            nbs = nbs + ghost[pl.ds(pl.multiple_of(48 * slot + base, 8), 8), :]
            here = (slot, pl.ds(pl.multiple_of(base + 8, 8), 8), pl.ds(EDGE, ROW))
            old = g[here]
            rows_here = pl.ds(base, 8)
            g[here] = old + fr2[slot, rows_here, :] * (c - old) + frc[slot, rows_here, :] * (nbs - 6.0 * c)

    def restrict(f, step):
        lefts = []
        for slot in range(2):
            high, low = split(f[slot, pl.ds(8, FINE), pl.ds(EDGE, ROW)])
            part = dot(down[...], jnp.concatenate([high, low], axis=0))
            lefts.extend(split(part))
        means = dot(jnp.concatenate(lefts, axis=0), gather[...])
        for slot in range(2):
            mean = (means[32 * slot:32 * slot + 16] + means[32 * slot + 16:32 * slot + 32]) * (1.0 / 27.0)
            rest_out[step, slot] = mean
            rest_in[step, 0, slot] = mean
        for j in range(1, 4):
            rest_copy(step, j).start()

    def insert(new, step):
        for j in range(1, 4):
            rest_copy(step, j).wait_recv()

        @pl.loop(0, 4)
        def _(entry):
            value = rest_in[step, 0, 0]
            for j in range(4):
                for slot in range(2):
                    hit = inter[0, 0, entry] == 2 * (quad[j][0] * nb + quad[j][1]) + slot
                    value = jnp.where(hit, rest_in[step, j, slot], value)
            high, low = split(value)
            left = [(dot(rep[...], part) * own[...]).astype(bf16) for part in (high, low)]
            blocks[entry] = dot(jnp.concatenate(left, axis=1), tile[...])

        place = lax.div(lane16, 16)

        @pl.loop(0, 4)
        def _(i):
            for j in range(4):
                masks = []
                for entry in range(4):
                    hit = (inter[0, 0, entry] >= 0) & (inter[0, 1, entry] == 16 * i) & (inter[0, 2, entry] == 16 * j)
                    at = jnp.where(hit, lax.div(inter[0, 3, entry], 16), -1)
                    masks.append(place == at)

                @pl.loop(0, 16)
                def _(x):
                    where = (16 * i + x + 1, pl.ds(8 + 16 * j, 16), slice(None))
                    value = new[where]
                    for entry in range(4):
                        block = blocks[entry, pl.ds(pl.multiple_of(16 * x, 16), 16), :]
                        value = jnp.where(masks[entry], block, value)
                    new[where] = value

    loads[0].wait()
    send_halo(0, p0)
    for load in loads[1:]:
        load.wait()

    @pl.loop(0, nx)
    def _(x):
        r = 1.0 / (1.0 + r2[x])
        r2[x] = 2.0 * r
        rc[x] = rc[x] * r

    for slot in range(2):
        @pl.loop(0, 6)
        def _(i):
            at = (slot, pl.ds(pl.multiple_of(8 * i, 8), 8), slice(None))
            r = 1.0 / (1.0 + fr2[at])
            fr2[at] = 2.0 * r
            frc[at] = frc[at] * r

    f, g = fa, fb
    stores = []
    for step in range(STEPS):
        field, new = fields[step], fields[step + 1]
        if step == 0:
            def before(x):
                return q0[x]
        else:
            def before(x):
                return p0[x + 1, pl.ds(8, ny), :]
            send_halo(2, field)
        take_halo(2 * step, field)
        send_faces(2 * step, field)
        coarse_update(new, field, before)
        send_halo(2 * step + 1, new)
        take_faces(2 * step)
        make_ghosts(f, step, 0.0)
        fine_update(f, g, 0)
        take_halo(2 * step + 1, new)
        send_faces(2 * step + 1, new)
        fine_update(f, g, 1)
        f, g = g, f
        take_faces(2 * step + 1)
        for sub in (1, 2):
            make_ghosts(f, step, sub / 3.0)
            for slot in range(2):
                fine_update(f, g, slot)
            f, g = g, f
        restrict(f, step)
        if step == STEPS - 1:
            stores.append(pltpu.make_async_copy(f.at[fmid], fnext_h, store_sem.at[0]))
            stores.append(pltpu.make_async_copy(g.at[fmid], flast_h, store_sem.at[1]))
            for store in stores[-2:]:
                store.start()
        insert(new, step)
        out = next_h if step == STEPS - 1 else last_h
        store = pltpu.make_async_copy(new.at[mid], out, store_sem.at[2 + step])
        if step == STEPS - 1:
            store.start()
            stores.append(store)
        else:
            last_store = store
            last_store.start()

    for phase in range(4):
        for side in range(4):
            @pl.when(exists[side])
            def _(phase=phase, side=side):
                halo_copy(phase, side).wait_send()
        for j in range(1, 4):
            face_copy(phase, j).wait_send()
    for step in range(STEPS):
        for j in range(1, 4):
            rest_copy(step, j).wait_send()
    last_store.wait()
    for store in stores:
        store.wait()


def on_device(nt, nb, *args):
    coarse, fine = args[:4], args[4:8]
    anchor, inter = args[8], args[9]
    consts = [jnp.asarray(c) for c in constants()]
    f32 = jnp.float32
    smem = pl.BlockSpec(memory_space=pltpu.SMEM)
    vmem = pl.BlockSpec(memory_space=pltpu.VMEM)
    hbm = pl.BlockSpec(memory_space=pl.ANY)
    shape_c, shape_f = coarse[0].shape, fine[0].shape
    dma = pltpu.SemaphoreType.DMA
    return pl.pallas_call(
        functools.partial(kernel, nt, nb),
        out_shape=[jax.ShapeDtypeStruct(s, f32) for s in (shape_c, shape_c, shape_f, shape_f)],
        in_specs=[smem, smem] + [hbm] * 8 + [vmem] * len(consts),
        out_specs=[hbm] * 4,
        scratch_shapes=[
            pltpu.VMEM((66, 80, 128), f32),
            pltpu.VMEM((66, 80, 128), f32),
            pltpu.VMEM((66, 80, 128), f32),
            pltpu.VMEM((64, 64, 128), f32),
            pltpu.VMEM((64, 64, 128), f32),
            pltpu.VMEM((64, 64, 128), f32),
            pltpu.VMEM((2, 64, ROW + 2 * EDGE), f32),
            pltpu.VMEM((2, 64, ROW + 2 * EDGE), f32),
            pltpu.VMEM((2, FINE, ROW), f32),
            pltpu.VMEM((2, FINE, ROW), f32),
            pltpu.VMEM((4, 4, 64, 128), f32),
            pltpu.VMEM((4, 4, 64, 128), f32),
            pltpu.VMEM((4, 3, 2, 48, 128), f32),
            pltpu.VMEM((4, 4, 2, 48, 128), f32),
            pltpu.VMEM((2, 2, 16, 256), f32),
            pltpu.VMEM((2, 4, 2, 16, 256), f32),
            pltpu.VMEM((160, ROW), f32),
            pltpu.VMEM((4, 256, 128), f32),
            pltpu.VMEM((4, 256, 128), f32),
            pltpu.VMEM((4, 64, 128), f32),
            dma((4, 4)), dma((4, 4)), dma((4, 3)), dma((4, 3)), dma((2, 3)), dma((2, 3)),
            dma((8,)), dma((4,)),
        ],
        compiler_params=pltpu.CompilerParams(
            collective_id=0, has_side_effects=True, vmem_limit_bytes=56 * 1024 * 1024
        ),
        cost_estimate=pl.CostEstimate(flops=40_000_000, bytes_accessed=20_000_000, transcendentals=0),
        name="wave",
    )(inter, anchor, *coarse, *fine, *consts)


def solution(mesh):
    whole = ("tile", "bulk")
    c, f = P("tile", "bulk", None), P(whole, None, None)
    return jax.shard_map(
        functools.partial(on_device, mesh.shape["tile"], mesh.shape["bulk"]),
        mesh=mesh,
        in_specs=(c, c, c, c, f, f, f, f, P(whole, None), f),
        out_specs=(c, c, f, f),
        check_vma=False,
    )
```

```python
import functools

import jax
import jax.numpy as jnp
import ml_dtypes
import numpy as np
from jax import lax
from jax.experimental import pallas as pl
from jax.experimental.pallas import tpu as pltpu
from jax.sharding import PartitionSpec as P

STEPS = 2
MESH = pl.DeviceIdType.MESH
BC, FINE = 16, 48
ROW = FINE * FINE
COLS = ROW // 128
bf16 = jnp.bfloat16


def constants():
    flat = np.arange(ROW)
    y, z = flat // FINE, flat % FINE
    group = np.arange(BC)[:, None]
    spread = np.zeros((128, ROW), np.float32)
    spread[0:16] = (y == 0) & (z // 3 == group)
    spread[16:32] = (y == FINE - 1) & (z // 3 == group)
    spread[32:48] = (z == 0) & (y // 3 == group)
    spread[48:64] = (z == FINE - 1) & (y // 3 == group)
    spread[64:80] = z // 3 == group
    spread = np.concatenate([spread, spread], 0)
    up = np.zeros((160, 96), np.float32)
    for box in range(2):
        for x in range(FINE):
            up[box * 48 + x, box * 48 + x // 3] = 1
        for r in range(32):
            up[96 + box * 32 + r, box * 48 + 16 + r] = 1
    rows = (y // 3 == group).astype(np.float32)
    rows = rows.reshape(BC, COLS, 128).transpose(1, 0, 2)
    inside = np.stack([np.tile(z != 0, (8, 1)), np.tile(z != FINE - 1, (8, 1))]).astype(np.float32)
    inside = inside.reshape(2, 8, COLS, 128)[:, :, :3].transpose(2, 0, 1, 3)
    down = np.zeros((16, 96), np.float32)
    for x in range(FINE):
        down[x // 3, x] = 1
        down[x // 3, 48 + x] = 1
    gather = np.zeros((ROW, 256), np.float32)
    gather[flat, (y // 3) * 16 + z // 3] = 1
    rep = np.zeros((256, 16), np.float32)
    rep[np.arange(256), np.arange(256) // 16] = 1
    own = (np.arange(256)[:, None] % 16 == np.arange(256)[None] // 16).astype(np.float32)
    tile = (np.arange(256)[:, None] % 16 == np.arange(128)[None] % 16).astype(np.float32)
    tile = np.concatenate([tile, tile], 0)
    half = ml_dtypes.bfloat16
    return [
        spread.astype(half), up.astype(half), rows, inside, down.astype(half),
        gather.astype(half), rep.astype(half), own, tile.astype(half),
    ]


def split(value):
    high = value.astype(bf16)
    low = (value - high.astype(jnp.float32)).astype(bf16)
    return high, low


def dot(a, b):
    return jnp.dot(a, b, preferred_element_type=jnp.float32)


def kernel(
    nt, nb,
    inter, anchor,
    now_h, before_h, courant_h, absorb_h, fnow_h, fbefore_h, fcourant_h, fabsorb_h,
    spread, up, rows, inside, down, gather, rep, own, tile,
    next_h, last_h, fnext_h, flast_h,
    p0, p1, p2, q0, rc, r2, fa, fb, frc, fr2,
    halo_out, halo_in, face_out, face_in, rest_out, rest_in,
    ghost, blocks, cubes, edges, picks, windows,
    halo_ss, halo_rs, face_ss, face_rs, rest_ss, rest_rs, load_sem, store_sem,
):
    t, b = lax.axis_index("tile"), lax.axis_index("bulk")
    fields = [p0, p1, p2]
    nx, ny = 64, 64

    exists = [t > 0, t < nt - 1, b > 0, b < nb - 1]
    missing = [t == 0, t == nt - 1, b == 0, b == nb - 1]
    beside = [(t - 1, b), (t + 1, b), (t, b - 1), (t, b + 1)]
    b_other = b + 1 - 2 * lax.rem(b, 2)
    t_other = lax.rem(t + nt // 2, nt)
    quad = [(t, b), (t, b_other), (t_other, b), (t_other, b_other)]

    mid = (pl.ds(1, nx), pl.ds(8, ny), slice(None))
    loads = [
        pltpu.make_async_copy(src, dst, load_sem.at[i])
        for i, (src, dst) in enumerate([
            (now_h, p0.at[mid]),
            (before_h, q0),
            (courant_h, rc),
            (absorb_h, r2),
        ] + [
            (src.at[:, :, pl.ds(128 * c, 128)], dst)
            for c in range(COLS)
            for src, dst in (
                (fcourant_h, frc.at[:, c]),
                (fabsorb_h, fr2.at[:, c]),
                (fnow_h, fa.at[:, c + 1, pl.ds(8, FINE), :]),
                (fbefore_h, fb.at[:, c + 1, pl.ds(8, FINE), :]),
            )
        ])
    ]
    for load in loads:
        load.start()

    barrier = pltpu.get_barrier_semaphore()
    for have, device in zip(exists, beside):
        @pl.when(have)
        def _(device=device):
            pl.semaphore_signal(barrier, inc=1, device_id=device, device_id_type=MESH)
    for device in quad[2:]:
        pl.semaphore_signal(barrier, inc=1, device_id=device, device_id_type=MESH)
    peers = jnp.int32(2)
    for have in exists:
        peers = peers + jnp.where(have, 1, 0)
    pl.semaphore_wait(barrier, peers)

    zero_side = jnp.zeros((2, 64, 128), jnp.float32)
    for buf in (fa, fb):
        buf[:, 0] = zero_side
        buf[:, COLS + 1] = zero_side

    lane = lax.broadcasted_iota(jnp.int32, (64, 128), 1)
    not_first, not_last = lane != 0, lane != 127

    def halo_wait(phase, side):
        return pltpu.make_async_remote_copy(
            src_ref=halo_out.at[phase, side],
            dst_ref=halo_in.at[phase, side],
            send_sem=halo_ss.at[phase, side],
            recv_sem=halo_rs.at[phase, side],
            device_id=beside[side],
            device_id_type=MESH,
        )

    def halo_copy(phase, side):
        return pltpu.make_async_remote_copy(
            src_ref=halo_out.at[phase, side],
            dst_ref=halo_in.at[phase, side ^ 1],
            send_sem=halo_ss.at[phase, side],
            recv_sem=halo_rs.at[phase, side ^ 1],
            device_id=beside[side],
            device_id_type=MESH,
        )

    def send_halo(phase, field):
        halo_out[phase, 0] = field[1, pl.ds(8, ny), :]
        halo_out[phase, 1] = field[nx, pl.ds(8, ny), :]
        halo_out[phase, 2] = field[pl.ds(1, nx), 8, :]
        halo_out[phase, 3] = field[pl.ds(1, nx), 7 + ny, :]
        for side in range(4):
            @pl.when(exists[side])
            def _(side=side):
                halo_copy(phase, side).start()

    def take_halo(phase, field):
        for side in range(4):
            @pl.when(exists[side])
            def _(side=side):
                halo_wait(phase, side).wait_recv()

            @pl.when(missing[side])
            def _(side=side):
                halo_in[phase, side] = jnp.zeros((64, 128), jnp.float32)
        field[0, pl.ds(8, ny), :] = halo_in[phase, 0]
        field[nx + 1, pl.ds(8, ny), :] = halo_in[phase, 1]
        field[pl.ds(1, nx), 7, :] = halo_in[phase, 2]
        field[pl.ds(1, nx), 8 + ny, :] = halo_in[phase, 3]

    def face_copy(phase, j):
        return pltpu.make_async_remote_copy(
            src_ref=face_out.at[phase, j - 1],
            dst_ref=face_in.at[phase, j],
            send_sem=face_ss.at[phase, j - 1],
            recv_sem=face_rs.at[phase, j - 1],
            device_id=quad[j],
            device_id_type=MESH,
        )

    def rest_copy(step, j):
        return pltpu.make_async_remote_copy(
            src_ref=rest_out.at[step],
            dst_ref=rest_in.at[step, j],
            send_sem=rest_ss.at[step, j - 1],
            recv_sem=rest_rs.at[step, j - 1],
            device_id=quad[j],
            device_id_type=MESH,
        )

    lane16 = lax.broadcasted_iota(jnp.int32, (16, 128), 1)
    z_in = lax.broadcasted_iota(jnp.int32, (256, 128), 0)
    z_in = lax.rem(z_in, 128)
    z_out = lax.broadcasted_iota(jnp.int32, (256, 128), 1)
    y_row = lax.broadcasted_iota(jnp.int32, (16, 16, 128), 1)
    y_lane = lax.rem(lax.broadcasted_iota(jnp.int32, (16, 16, 128), 2), 16)

    at = [4 * lax.div(inter[0, 1, e], 16) + lax.div(inter[0, 2, e], 16) for e in range(4)]
    spots = [jnp.full((16, 128), a, jnp.int32) for a in at]

    def choose(load, height, store):
        values = [None] * 4
        for i in range(4):
            for j in range(4):
                value = load(i, j)
                for e in range(4):
                    if i + j == 0:
                        values[e] = value
                    else:
                        values[e] = jnp.where(spots[e][:height] == 4 * i + j, value, values[e])
        for e in range(4):
            store(e, values[e])

    def collect(field):
        def to_edges(row, height):
            def store(e, value):
                edges[e, pl.ds(row, height), :] = value
            return store

        choose(lambda i, j: field[16 * i, pl.ds(8 + 16 * j, 16), :], 16, to_edges(32, 16))
        choose(lambda i, j: field[16 * i + 17, pl.ds(8 + 16 * j, 16), :], 16, to_edges(48, 16))

        choose(lambda i, j: field[pl.ds(16 * i + 1, 16), 7 + 16 * j, :], 16, to_edges(0, 16))
        choose(lambda i, j: field[pl.ds(16 * i + 1, 16), 24 + 16 * j, :], 16, to_edges(16, 16))

    def prepare_faces(field):
        @pl.loop(0, 16)
        def _(u):
            def to_cubes(e, value):
                cubes[e, pl.ds(pl.multiple_of(16 * u, 16), 16), :] = value
            choose(lambda i, j: field[16 * i + 1 + u, pl.ds(8 + 16 * j, 16), :], 16, to_cubes)

        @pl.loop(0, 4)
        def _(entry):
            high, low = split(cubes[entry])
            zs = dot(jnp.concatenate([high, low], axis=1), picks[entry]).reshape(16, 16, 128)
            blocks[entry, pl.ds(0, 16), :] = jnp.sum(jnp.where(y_row == y_lane, zs, 0.0), axis=1)

    def make_picks():
        @pl.loop(0, 4)
        def _(entry):
            z0 = inter[0, 3, entry]
            pick = ((z_in == z0 - 1) & (z_out >= 32) & (z_out < 48)) | (
                (z_in == z0 + 16) & (z_out >= 48) & (z_out < 64)
            )
            picks[entry] = jnp.where(pick, 1.0, 0.0).astype(bf16)
            windows[entry] = jnp.where(z_in == z0 + lax.rem(z_out, 16), 1.0, 0.0).astype(bf16)

    def faces_of(ref, entry):
        high, low = split(edges[entry])
        flat = dot(jnp.concatenate([high, low], axis=1), windows[entry])
        zs = ref[pl.ds(0, 16), :]
        first = jnp.where(lane16 < 16, flat[0:16], jnp.where(lane16 < 32, flat[16:32], zs))
        x_lanes = (lane16 >= 64) & (lane16 < 80)
        ref[pl.ds(0, 16), :] = jnp.where(lane16 < 64, first, 0.0)
        ref[pl.ds(16, 16), :] = jnp.where(x_lanes, flat[32:48], 0.0)
        ref[pl.ds(32, 16), :] = jnp.where(x_lanes, flat[48:64], 0.0)

    def faces_for(j, slot):
        target = 2 * (quad[j][0] * nb + quad[j][1]) + slot
        value = blocks[0, pl.ds(0, 48), :]
        for entry in range(1, 4):
            hit = inter[0, 0, entry] == target
            value = jnp.where(hit, blocks[entry, pl.ds(0, 48), :], value)
        return value

    def send_faces(phase, field):
        collect(field)

        @pl.loop(0, 4)
        def _(entry):
            faces_of(blocks.at[entry, pl.ds(0, 48), :], entry)
        for j in range(1, 4):
            for slot in range(2):
                face_out[phase, j - 1, slot] = faces_for(j, slot)
            face_copy(phase, j).start()
        for slot in range(2):
            face_in[phase, 0, slot] = faces_for(0, slot)

    def take_faces(phase):
        for j in range(1, 4):
            face_copy(phase, j).wait_recv()

    def source_of(slot):
        away_t = jnp.where(lax.div(anchor[slot, 0], 64) == t, 0, 2)
        away_b = jnp.where(lax.div(anchor[slot, 1], 64) == b, 0, 1)
        return away_t + away_b

    sources = [source_of(slot) for slot in range(2)]

    def arrived(phase, slot):
        value = face_in[phase, 0, slot]
        for j in range(1, 4):
            value = jnp.where(sources[slot] == j, face_in[phase, j, slot], value)
        return value

    def coarse_update(new, field, before):
        @pl.loop(0, nx)
        def _(x):
            c = field[x + 1, pl.ds(8, ny), :]
            nbs = field[x, pl.ds(8, ny), :] + field[x + 2, pl.ds(8, ny), :]
            nbs = nbs + field[x + 1, pl.ds(7, ny), :] + field[x + 1, pl.ds(9, ny), :]
            nbs = nbs + jnp.where(not_first, pltpu.roll(c, 1, 1), 0.0)
            nbs = nbs + jnp.where(not_last, pltpu.roll(c, 127, 1), 0.0)
            old = before(x)
            new[x + 1, pl.ds(8, ny), :] = old + r2[x] * (c - old) + rc[x] * (nbs - 6.0 * c)

    def make_ghosts(f, phase, weight):
        parts = []
        for slot in range(2):
            q = arrived(2 * phase, slot)
            if weight:
                q = q + weight * (arrived(2 * phase + 1, slot) - q)
            parts.append(q)
        high, low = split(jnp.concatenate(parts, axis=0))
        left = dot(up[...], jnp.concatenate([high, low], axis=1)).astype(bf16)

        @pl.loop(0, 9)
        def _(c):
            both = dot(left, spread[:, pl.ds(pl.multiple_of(c * 256, 256), 256)])
            for half in range(2):
                col = 2 * c + half
                part = both[:, 128 * half:128 * half + 128]
                ghost[col] = part[:96]
                for slot in range(2):
                    for k in range(2):
                        first = 96 + 32 * slot + 16 * k
                        face = part[first:first + 16] * rows[col]
                        f[slot, col + 1, pl.ds(7 + 49 * k, 1), :] = jnp.sum(face, axis=0, keepdims=True)

    lane8 = lax.broadcasted_iota(jnp.int32, (8, 128), 1)
    under = {shift: lane8 < shift for shift in (1, 48, 80, 127)}

    def fine_update(f, g, slot):
        @pl.loop(0, 6)
        def _(i):
            base = pl.multiple_of(8 * i, 8)

            def turned(col):
                value = f[slot, col, pl.ds(pl.multiple_of(base + 8, 8), 8), :]
                return value, {shift: pltpu.roll(value, shift, 1) for shift in under}

            _, before = turned(0)
            c, here = turned(1)
            for col in range(COLS):
                later, after = turned(col + 2)
                nbs = f[slot, col + 1, pl.ds(base + 7, 8), :] + f[slot, col + 1, pl.ds(base + 9, 8), :]
                nbs = nbs + jnp.where(under[48], before[48], here[48])
                nbs = nbs + jnp.where(under[80], here[80], after[80])
                nbs = nbs + jnp.where(under[1], before[1], here[1]) * inside[col % 3, 0]
                nbs = nbs + jnp.where(under[127], here[127], after[127]) * inside[col % 3, 1]
                nbs = nbs + ghost[col, pl.ds(pl.multiple_of(48 * slot + base, 8), 8), :]
                place = (slot, col + 1, pl.ds(pl.multiple_of(base + 8, 8), 8), slice(None))
                old = g[place]
                coef = (slot, col, pl.ds(base, 8), slice(None))
                g[place] = old + fr2[coef] * (c - old) + frc[coef] * (nbs - 6.0 * c)
                before, here, c = here, after, later

    def restrict(f, step):
        means = jnp.zeros((64, 256), jnp.float32)
        for pair in range(COLS // 2):
            lefts = []
            for slot in range(2):
                cols = [f[slot, 2 * pair + 1 + k, pl.ds(8, FINE), :] for k in range(2)]
                high, low = split(jnp.concatenate(cols, axis=1))
                lefts.extend(split(dot(down[...], jnp.concatenate([high, low], axis=0))))
            means = means + dot(jnp.concatenate(lefts, axis=0), gather[pl.ds(256 * pair, 256), :])
        for slot in range(2):
            mean = (means[32 * slot:32 * slot + 16] + means[32 * slot + 16:32 * slot + 32]) * (1.0 / 27.0)
            rest_out[step, slot] = mean
            rest_in[step, 0, slot] = mean
        for j in range(1, 4):
            rest_copy(step, j).start()

    def insert(new, step):
        for j in range(1, 4):
            rest_copy(step, j).wait_recv()

        @pl.loop(0, 4)
        def _(entry):
            value = rest_in[step, 0, 0]
            for j in range(4):
                for slot in range(2):
                    hit = inter[0, 0, entry] == 2 * (quad[j][0] * nb + quad[j][1]) + slot
                    value = jnp.where(hit, rest_in[step, j, slot], value)
            high, low = split(value)
            left = [(dot(rep[...], part) * own[...]).astype(bf16) for part in (high, low)]
            blocks[entry] = dot(jnp.concatenate(left, axis=1), tile[...])

        place = lax.div(lane16, 16)

        @pl.loop(0, 4)
        def _(i):
            for j in range(4):
                masks = []
                for entry in range(4):
                    hit = (inter[0, 0, entry] >= 0) & (inter[0, 1, entry] == 16 * i) & (inter[0, 2, entry] == 16 * j)
                    at = jnp.where(hit, lax.div(inter[0, 3, entry], 16), -1)
                    masks.append(place == at)

                @pl.loop(0, 16)
                def _(x):
                    where = (16 * i + x + 1, pl.ds(8 + 16 * j, 16), slice(None))
                    value = new[where]
                    for entry in range(4):
                        block = blocks[entry, pl.ds(pl.multiple_of(16 * x, 16), 16), :]
                        value = jnp.where(masks[entry], block, value)
                    new[where] = value

    loads[0].wait()
    send_halo(0, p0)
    make_picks()
    prepare_faces(p0)
    for load in loads[1:4]:
        load.wait()

    @pl.loop(0, nx)
    def _(x):
        r = 1.0 / (1.0 + r2[x])
        r2[x] = 2.0 * r
        rc[x] = rc[x] * r

    for load in loads[4:]:
        load.wait()

    for slot in range(2):
        @pl.loop(0, COLS)
        def _(c):
            r = 1.0 / (1.0 + fr2[slot, c])
            fr2[slot, c] = 2.0 * r
            frc[slot, c] = frc[slot, c] * r

    f, g = fa, fb
    stores = []
    for step in range(STEPS):
        field, new = fields[step], fields[step + 1]
        if step == 0:
            def before(x):
                return q0[x]
        else:
            def before(x):
                return p0[x + 1, pl.ds(8, ny), :]
            send_halo(2, field)
            prepare_faces(field)
        take_halo(2 * step, field)
        send_faces(2 * step, field)
        coarse_update(new, field, before)
        send_halo(2 * step + 1, new)
        take_faces(2 * step)
        make_ghosts(f, step, 0.0)
        fine_update(f, g, 0)
        prepare_faces(new)
        take_halo(2 * step + 1, new)
        send_faces(2 * step + 1, new)
        fine_update(f, g, 1)
        f, g = g, f
        take_faces(2 * step + 1)
        for sub in (1, 2):
            make_ghosts(f, step, sub / 3.0)
            for slot in range(2):
                fine_update(f, g, slot)
            f, g = g, f
        restrict(f, step)
        if step == STEPS - 1:
            for k, (src, dst) in enumerate([(f, fnext_h), (g, flast_h)]):
                for c in range(COLS):
                    store = pltpu.make_async_copy(
                        src.at[:, c + 1, pl.ds(8, FINE), :],
                        dst.at[:, :, pl.ds(128 * c, 128)],
                        store_sem.at[2 + k * COLS + c],
                    )
                    store.start()
                    stores.append(store)
        insert(new, step)
        out = next_h if step == STEPS - 1 else last_h
        store = pltpu.make_async_copy(new.at[mid], out, store_sem.at[step])
        if step == STEPS - 1:
            store.start()
            stores.append(store)
        else:
            last_store = store
            last_store.start()

    for phase in range(4):
        for side in range(4):
            @pl.when(exists[side])
            def _(phase=phase, side=side):
                halo_copy(phase, side).wait_send()
        for j in range(1, 4):
            face_copy(phase, j).wait_send()
    for step in range(STEPS):
        for j in range(1, 4):
            rest_copy(step, j).wait_send()
    last_store.wait()
    for store in stores:
        store.wait()


def hand_over(*refs):
    sources, targets, sems = refs[:4], refs[4:8], refs[8]
    copies = []
    for src, dst in zip(sources, targets):
        parts = 4 if src.shape[0] == 64 else 2
        rows = src.shape[0] // parts
        for k in range(parts):
            at = pl.ds(k * rows, rows)
            copies.append(pltpu.make_async_copy(src.at[at], dst.at[at], sems.at[len(copies)]))
    for copy in copies:
        copy.start()
    for copy in copies:
        copy.wait()


def on_device(nt, nb, *args):
    coarse, fine = args[:4], args[4:8]
    anchor, inter = args[8], args[9]
    consts = [jnp.asarray(c) for c in constants()]
    f32 = jnp.float32
    smem = pl.BlockSpec(memory_space=pltpu.SMEM)
    vmem = pl.BlockSpec(memory_space=pltpu.VMEM)
    hbm = pl.BlockSpec(memory_space=pl.ANY)
    shape_c, shape_f = coarse[0].shape, fine[0].shape
    dma = pltpu.SemaphoreType.DMA
    outs = pl.pallas_call(
        functools.partial(kernel, nt, nb),
        out_shape=[jax.ShapeDtypeStruct(s, f32) for s in (shape_c, shape_c, shape_f, shape_f)],
        in_specs=[smem, smem] + [hbm] * 8 + [vmem] * len(consts),
        out_specs=[hbm] * 4,
        scratch_shapes=[
            pltpu.VMEM((66, 80, 128), f32),
            pltpu.VMEM((66, 80, 128), f32),
            pltpu.VMEM((66, 80, 128), f32),
            pltpu.VMEM((64, 64, 128), f32),
            pltpu.VMEM((64, 64, 128), f32),
            pltpu.VMEM((64, 64, 128), f32),
            pltpu.VMEM((2, COLS + 2, 64, 128), f32),
            pltpu.VMEM((2, COLS + 2, 64, 128), f32),
            pltpu.VMEM((2, COLS, FINE, 128), f32),
            pltpu.VMEM((2, COLS, FINE, 128), f32),
            pltpu.VMEM((4, 4, 64, 128), f32),
            pltpu.VMEM((4, 4, 64, 128), f32),
            pltpu.VMEM((4, 3, 2, 48, 128), f32),
            pltpu.VMEM((4, 4, 2, 48, 128), f32),
            pltpu.VMEM((2, 2, 16, 256), f32),
            pltpu.VMEM((2, 4, 2, 16, 256), f32),
            pltpu.VMEM((COLS, 96, 128), f32),
            pltpu.VMEM((4, 256, 128), f32),
            pltpu.VMEM((4, 256, 128), f32),
            pltpu.VMEM((4, 64, 128), f32),
            pltpu.VMEM((4, 256, 128), bf16),
            pltpu.VMEM((4, 256, 128), bf16),
            dma((4, 4)), dma((4, 4)), dma((4, 3)), dma((4, 3)), dma((2, 3)), dma((2, 3)),
            dma((4 + 4 * COLS,)), dma((2 + 2 * COLS,)),
        ],
        compiler_params=pltpu.CompilerParams(
            collective_id=0, has_side_effects=True, vmem_limit_bytes=56 * 1024 * 1024
        ),
        cost_estimate=pl.CostEstimate(flops=40_000_000, bytes_accessed=20_000_000, transcendentals=0),
        name="wave",
    )(inter, anchor, *coarse, *fine, *consts)
    return pl.pallas_call(
        hand_over,
        out_shape=[jax.ShapeDtypeStruct(o.shape, f32) for o in outs],
        in_specs=[hbm] * 4,
        out_specs=[hbm] * 4,
        scratch_shapes=[dma((12,))],
        name="hand_over",
    )(*outs)


def solution(mesh):
    whole = ("tile", "bulk")
    c, f = P("tile", "bulk", None), P(whole, None, None)
    return jax.shard_map(
        functools.partial(on_device, mesh.shape["tile"], mesh.shape["bulk"]),
        mesh=mesh,
        in_specs=(c, c, c, c, f, f, f, f, P(whole, None), f),
        out_specs=(c, c, f, f),
        check_vma=False,
    )
```

```python
import functools

import jax
import jax.numpy as jnp
import ml_dtypes
import numpy as np
from jax import lax
from jax.experimental import pallas as pl
from jax.experimental.pallas import tpu as pltpu
from jax.sharding import PartitionSpec as P

STEPS = 2
MESH = pl.DeviceIdType.MESH
BC, FINE = 16, 48
ROW = FINE * FINE
COLS = ROW // 128
bf16 = jnp.bfloat16


def constants():
    flat = np.arange(ROW)
    y, z = flat // FINE, flat % FINE
    group = np.arange(BC)[:, None]
    spread = np.zeros((128, ROW), np.float32)
    spread[0:16] = (y == 0) & (z // 3 == group)
    spread[16:32] = (y == FINE - 1) & (z // 3 == group)
    spread[32:48] = (z == 0) & (y // 3 == group)
    spread[48:64] = (z == FINE - 1) & (y // 3 == group)
    spread[64:80] = z // 3 == group
    spread = np.concatenate([spread, spread], 0)
    up = np.zeros((160, 96), np.float32)
    for box in range(2):
        for x in range(FINE):
            up[box * 48 + x, box * 48 + x // 3] = 1
        for r in range(32):
            up[96 + box * 32 + r, box * 48 + 16 + r] = 1
    rows = (y // 3 == group).astype(np.float32)
    rows = rows.reshape(BC, COLS, 128).transpose(1, 0, 2)
    inside = np.stack([np.tile(z != 0, (8, 1)), np.tile(z != FINE - 1, (8, 1))]).astype(np.float32)
    inside = inside.reshape(2, 8, COLS, 128)[:, :, :3].transpose(2, 0, 1, 3)
    down = np.zeros((16, 96), np.float32)
    for x in range(FINE):
        down[x // 3, x] = 1
        down[x // 3, 48 + x] = 1
    gather = np.zeros((ROW, 256), np.float32)
    gather[flat, (y // 3) * 16 + z // 3] = 1
    rep = np.zeros((256, 16), np.float32)
    rep[np.arange(256), np.arange(256) // 16] = 1
    own = (np.arange(256)[:, None] % 16 == np.arange(256)[None] // 16).astype(np.float32)
    tile = (np.arange(256)[:, None] % 16 == np.arange(128)[None] % 16).astype(np.float32)
    tile = np.concatenate([tile, tile], 0)
    half = ml_dtypes.bfloat16
    return [
        spread.astype(half), up.astype(half), rows, inside, down.astype(half),
        gather.astype(half), rep.astype(half), own, tile.astype(half),
    ]


def split(value):
    high = value.astype(bf16)
    low = (value - high.astype(jnp.float32)).astype(bf16)
    return high, low


def dot(a, b):
    return jnp.dot(a, b, preferred_element_type=jnp.float32)


def kernel(
    nt, nb,
    inter, anchor,
    now_h, before_h, courant_h, absorb_h, fnow_h, fbefore_h, fcourant_h, fabsorb_h,
    spread, up, rows, inside, down, gather, rep, own, tile,
    next_h, last_h, fnext_h, flast_h,
    p0, p1, p2, q0, rc, r2, fa, fb, frc, fr2,
    halo_out, halo_in, face_out, face_in, rest_out, rest_in,
    ghost, blocks, cubes, edges, picks, windows,
    halo_ss, halo_rs, face_ss, face_rs, rest_ss, rest_rs, load_sem, store_sem,
):
    t, b = lax.axis_index("tile"), lax.axis_index("bulk")
    fields = [p0, p1, p2]
    nx, ny = 64, 64

    exists = [t > 0, t < nt - 1, b > 0, b < nb - 1]
    missing = [t == 0, t == nt - 1, b == 0, b == nb - 1]
    beside = [(t - 1, b), (t + 1, b), (t, b - 1), (t, b + 1)]
    b_other = b + 1 - 2 * lax.rem(b, 2)
    t_other = lax.rem(t + nt // 2, nt)
    quad = [(t, b), (t, b_other), (t_other, b), (t_other, b_other)]

    mid = (pl.ds(1, nx), pl.ds(8, ny), slice(None))
    loads = [
        pltpu.make_async_copy(src, dst, load_sem.at[i])
        for i, (src, dst) in enumerate([
            (now_h, p0.at[mid]),
            (before_h, q0),
            (courant_h, rc),
            (absorb_h, r2),
        ] + [
            (src.at[:, :, pl.ds(128 * c, 128)], dst)
            for c in range(COLS)
            for src, dst in (
                (fcourant_h, frc.at[:, c]),
                (fabsorb_h, fr2.at[:, c]),
                (fnow_h, fa.at[:, c + 1, pl.ds(8, FINE), :]),
                (fbefore_h, fb.at[:, c + 1, pl.ds(8, FINE), :]),
            )
        ])
    ]
    for load in loads:
        load.start()

    barrier = pltpu.get_barrier_semaphore()
    for have, device in zip(exists, beside):
        @pl.when(have)
        def _(device=device):
            pl.semaphore_signal(barrier, inc=1, device_id=device, device_id_type=MESH)
    for device in quad[2:]:
        pl.semaphore_signal(barrier, inc=1, device_id=device, device_id_type=MESH)
    peers = jnp.int32(2)
    for have in exists:
        peers = peers + jnp.where(have, 1, 0)
    pl.semaphore_wait(barrier, peers)

    zero_side = jnp.zeros((2, 64, 128), jnp.float32)
    for buf in (fa, fb):
        buf[:, 0] = zero_side
        buf[:, COLS + 1] = zero_side

    lane = lax.broadcasted_iota(jnp.int32, (64, 128), 1)
    not_first, not_last = lane != 0, lane != 127

    def halo_wait(phase, side):
        return pltpu.make_async_remote_copy(
            src_ref=halo_out.at[phase, side],
            dst_ref=halo_in.at[phase, side],
            send_sem=halo_ss.at[phase, side],
            recv_sem=halo_rs.at[phase, side],
            device_id=beside[side],
            device_id_type=MESH,
        )

    def halo_copy(phase, side):
        return pltpu.make_async_remote_copy(
            src_ref=halo_out.at[phase, side],
            dst_ref=halo_in.at[phase, side ^ 1],
            send_sem=halo_ss.at[phase, side],
            recv_sem=halo_rs.at[phase, side ^ 1],
            device_id=beside[side],
            device_id_type=MESH,
        )

    def send_halo(phase, field):
        halo_out[phase, 0] = field[1, pl.ds(8, ny), :]
        halo_out[phase, 1] = field[nx, pl.ds(8, ny), :]
        halo_out[phase, 2] = field[pl.ds(1, nx), 8, :]
        halo_out[phase, 3] = field[pl.ds(1, nx), 7 + ny, :]
        for side in range(4):
            @pl.when(exists[side])
            def _(side=side):
                halo_copy(phase, side).start()

    def take_halo(phase, field):
        for side in range(4):
            @pl.when(exists[side])
            def _(side=side):
                halo_wait(phase, side).wait_recv()

            @pl.when(missing[side])
            def _(side=side):
                halo_in[phase, side] = jnp.zeros((64, 128), jnp.float32)
        field[0, pl.ds(8, ny), :] = halo_in[phase, 0]
        field[nx + 1, pl.ds(8, ny), :] = halo_in[phase, 1]
        field[pl.ds(1, nx), 7, :] = halo_in[phase, 2]
        field[pl.ds(1, nx), 8 + ny, :] = halo_in[phase, 3]

    def face_copy(phase, j):
        return pltpu.make_async_remote_copy(
            src_ref=face_out.at[phase, j - 1],
            dst_ref=face_in.at[phase, j],
            send_sem=face_ss.at[phase, j - 1],
            recv_sem=face_rs.at[phase, j - 1],
            device_id=quad[j],
            device_id_type=MESH,
        )

    def rest_copy(step, j):
        return pltpu.make_async_remote_copy(
            src_ref=rest_out.at[step],
            dst_ref=rest_in.at[step, j],
            send_sem=rest_ss.at[step, j - 1],
            recv_sem=rest_rs.at[step, j - 1],
            device_id=quad[j],
            device_id_type=MESH,
        )

    lane16 = lax.broadcasted_iota(jnp.int32, (16, 128), 1)
    z_in = lax.broadcasted_iota(jnp.int32, (256, 128), 0)
    z_in = lax.rem(z_in, 128)
    z_out = lax.broadcasted_iota(jnp.int32, (256, 128), 1)
    y_row = lax.broadcasted_iota(jnp.int32, (16, 16, 128), 1)
    y_lane = lax.rem(lax.broadcasted_iota(jnp.int32, (16, 16, 128), 2), 16)

    at = [4 * lax.div(inter[0, 1, e], 16) + lax.div(inter[0, 2, e], 16) for e in range(4)]
    spots = [jnp.full((16, 128), a, jnp.int32) for a in at]

    def choose(load, height, store):
        values = [None] * 4
        for i in range(4):
            for j in range(4):
                value = load(i, j)
                for e in range(4):
                    if i + j == 0:
                        values[e] = value
                    else:
                        values[e] = jnp.where(spots[e][:height] == 4 * i + j, value, values[e])
        for e in range(4):
            store(e, values[e])

    def collect(field):
        def to_edges(row, height):
            def store(e, value):
                edges[e, pl.ds(row, height), :] = value
            return store

        choose(lambda i, j: field[16 * i, pl.ds(8 + 16 * j, 16), :], 16, to_edges(32, 16))
        choose(lambda i, j: field[16 * i + 17, pl.ds(8 + 16 * j, 16), :], 16, to_edges(48, 16))

        choose(lambda i, j: field[pl.ds(16 * i + 1, 16), 7 + 16 * j, :], 16, to_edges(0, 16))
        choose(lambda i, j: field[pl.ds(16 * i + 1, 16), 24 + 16 * j, :], 16, to_edges(16, 16))

    def prepare_faces(field):
        @pl.loop(0, 16, unroll=2)
        def _(u):
            def to_cubes(e, value):
                cubes[e, pl.ds(pl.multiple_of(16 * u, 16), 16), :] = value
            choose(lambda i, j: field[16 * i + 1 + u, pl.ds(8 + 16 * j, 16), :], 16, to_cubes)

        @pl.loop(0, 4, unroll=4)
        def _(entry):
            high, low = split(cubes[entry])
            zs = dot(jnp.concatenate([high, low], axis=1), picks[entry]).reshape(16, 16, 128)
            blocks[entry, pl.ds(0, 16), :] = jnp.sum(jnp.where(y_row == y_lane, zs, 0.0), axis=1)

    def make_picks():
        @pl.loop(0, 4, unroll=4)
        def _(entry):
            z0 = inter[0, 3, entry]
            pick = ((z_in == z0 - 1) & (z_out >= 32) & (z_out < 48)) | (
                (z_in == z0 + 16) & (z_out >= 48) & (z_out < 64)
            )
            picks[entry] = jnp.where(pick, 1.0, 0.0).astype(bf16)
            windows[entry] = jnp.where(z_in == z0 + lax.rem(z_out, 16), 1.0, 0.0).astype(bf16)

    def faces_of(ref, entry):
        high, low = split(edges[entry])
        flat = dot(jnp.concatenate([high, low], axis=1), windows[entry])
        zs = ref[pl.ds(0, 16), :]
        first = jnp.where(lane16 < 16, flat[0:16], jnp.where(lane16 < 32, flat[16:32], zs))
        x_lanes = (lane16 >= 64) & (lane16 < 80)
        ref[pl.ds(0, 16), :] = jnp.where(lane16 < 64, first, 0.0)
        ref[pl.ds(16, 16), :] = jnp.where(x_lanes, flat[32:48], 0.0)
        ref[pl.ds(32, 16), :] = jnp.where(x_lanes, flat[48:64], 0.0)

    def faces_for(j, slot):
        target = 2 * (quad[j][0] * nb + quad[j][1]) + slot
        value = blocks[0, pl.ds(0, 48), :]
        for entry in range(1, 4):
            hit = inter[0, 0, entry] == target
            value = jnp.where(hit, blocks[entry, pl.ds(0, 48), :], value)
        return value

    def send_faces(phase, field):
        collect(field)

        @pl.loop(0, 4, unroll=4)
        def _(entry):
            faces_of(blocks.at[entry, pl.ds(0, 48), :], entry)
        for j in range(1, 4):
            for slot in range(2):
                face_out[phase, j - 1, slot] = faces_for(j, slot)
            face_copy(phase, j).start()
        for slot in range(2):
            face_in[phase, 0, slot] = faces_for(0, slot)

    def take_faces(phase):
        for j in range(1, 4):
            face_copy(phase, j).wait_recv()

    def source_of(slot):
        away_t = jnp.where(lax.div(anchor[slot, 0], 64) == t, 0, 2)
        away_b = jnp.where(lax.div(anchor[slot, 1], 64) == b, 0, 1)
        return away_t + away_b

    sources = [source_of(slot) for slot in range(2)]

    def arrived(phase, slot):
        value = face_in[phase, 0, slot]
        for j in range(1, 4):
            value = jnp.where(sources[slot] == j, face_in[phase, j, slot], value)
        return value

    def coarse_update(new, field, before):
        @pl.loop(0, nx, unroll=4)
        def _(x):
            c = field[x + 1, pl.ds(8, ny), :]
            nbs = field[x, pl.ds(8, ny), :] + field[x + 2, pl.ds(8, ny), :]
            nbs = nbs + field[x + 1, pl.ds(7, ny), :] + field[x + 1, pl.ds(9, ny), :]
            nbs = nbs + jnp.where(not_first, pltpu.roll(c, 1, 1), 0.0)
            nbs = nbs + jnp.where(not_last, pltpu.roll(c, 127, 1), 0.0)
            old = before(x)
            new[x + 1, pl.ds(8, ny), :] = old + r2[x] * (c - old) + rc[x] * (nbs - 6.0 * c)

    def make_ghosts(f, phase, weight):
        parts = []
        for slot in range(2):
            q = arrived(2 * phase, slot)
            if weight:
                q = q + weight * (arrived(2 * phase + 1, slot) - q)
            parts.append(q)
        high, low = split(jnp.concatenate(parts, axis=0))
        left = dot(up[...], jnp.concatenate([high, low], axis=1)).astype(bf16)

        @pl.loop(0, 9, unroll=9)
        def _(c):
            both = dot(left, spread[:, pl.ds(pl.multiple_of(c * 256, 256), 256)])
            for half in range(2):
                col = 2 * c + half
                part = both[:, 128 * half:128 * half + 128]
                ghost[col] = part[:96]
                for slot in range(2):
                    for k in range(2):
                        first = 96 + 32 * slot + 16 * k
                        face = part[first:first + 16] * rows[col]
                        f[slot, col + 1, pl.ds(7 + 49 * k, 1), :] = jnp.sum(face, axis=0, keepdims=True)

    lane8 = lax.broadcasted_iota(jnp.int32, (8, 128), 1)
    under = {shift: lane8 < shift for shift in (1, 48, 80, 127)}

    def fine_update(f, g, slot):
        @pl.loop(0, 6, unroll=2)
        def _(i):
            base = pl.multiple_of(8 * i, 8)

            def turned(col):
                value = f[slot, col, pl.ds(pl.multiple_of(base + 8, 8), 8), :]
                return value, {shift: pltpu.roll(value, shift, 1) for shift in under}

            _, before = turned(0)
            c, here = turned(1)
            for col in range(COLS):
                later, after = turned(col + 2)
                nbs = f[slot, col + 1, pl.ds(base + 7, 8), :] + f[slot, col + 1, pl.ds(base + 9, 8), :]
                nbs = nbs + jnp.where(under[48], before[48], here[48])
                nbs = nbs + jnp.where(under[80], here[80], after[80])
                nbs = nbs + jnp.where(under[1], before[1], here[1]) * inside[col % 3, 0]
                nbs = nbs + jnp.where(under[127], here[127], after[127]) * inside[col % 3, 1]
                nbs = nbs + ghost[col, pl.ds(pl.multiple_of(48 * slot + base, 8), 8), :]
                place = (slot, col + 1, pl.ds(pl.multiple_of(base + 8, 8), 8), slice(None))
                old = g[place]
                coef = (slot, col, pl.ds(base, 8), slice(None))
                g[place] = old + fr2[coef] * (c - old) + frc[coef] * (nbs - 6.0 * c)
                before, here, c = here, after, later

    def restrict(f, step):
        means = jnp.zeros((64, 256), jnp.float32)
        for pair in range(COLS // 2):
            lefts = []
            for slot in range(2):
                cols = [f[slot, 2 * pair + 1 + k, pl.ds(8, FINE), :] for k in range(2)]
                high, low = split(jnp.concatenate(cols, axis=1))
                lefts.extend(split(dot(down[...], jnp.concatenate([high, low], axis=0))))
            means = means + dot(jnp.concatenate(lefts, axis=0), gather[pl.ds(256 * pair, 256), :])
        for slot in range(2):
            mean = (means[32 * slot:32 * slot + 16] + means[32 * slot + 16:32 * slot + 32]) * (1.0 / 27.0)
            rest_out[step, slot] = mean
            rest_in[step, 0, slot] = mean
        for j in range(1, 4):
            rest_copy(step, j).start()

    def insert(new, step):
        for j in range(1, 4):
            rest_copy(step, j).wait_recv()

        @pl.loop(0, 4, unroll=4)
        def _(entry):
            value = rest_in[step, 0, 0]
            for j in range(4):
                for slot in range(2):
                    hit = inter[0, 0, entry] == 2 * (quad[j][0] * nb + quad[j][1]) + slot
                    value = jnp.where(hit, rest_in[step, j, slot], value)
            high, low = split(value)
            left = [(dot(rep[...], part) * own[...]).astype(bf16) for part in (high, low)]
            blocks[entry] = dot(jnp.concatenate(left, axis=1), tile[...])

        place = lax.div(lane16, 16)

        @pl.loop(0, 4)
        def _(i):
            for j in range(4):
                masks = []
                for entry in range(4):
                    hit = (inter[0, 0, entry] >= 0) & (inter[0, 1, entry] == 16 * i) & (inter[0, 2, entry] == 16 * j)
                    at = jnp.where(hit, lax.div(inter[0, 3, entry], 16), -1)
                    masks.append(place == at)

                @pl.loop(0, 16, unroll=16)
                def _(x):
                    where = (16 * i + x + 1, pl.ds(8 + 16 * j, 16), slice(None))
                    value = new[where]
                    for entry in range(4):
                        block = blocks[entry, pl.ds(pl.multiple_of(16 * x, 16), 16), :]
                        value = jnp.where(masks[entry], block, value)
                    new[where] = value

    loads[0].wait()
    send_halo(0, p0)
    make_picks()
    prepare_faces(p0)
    for load in loads[1:4]:
        load.wait()

    @pl.loop(0, nx, unroll=8)
    def _(x):
        r = 1.0 / (1.0 + r2[x])
        r2[x] = 2.0 * r
        rc[x] = rc[x] * r

    for load in loads[4:]:
        load.wait()

    for slot in range(2):
        @pl.loop(0, COLS, unroll=6)
        def _(c):
            r = 1.0 / (1.0 + fr2[slot, c])
            fr2[slot, c] = 2.0 * r
            frc[slot, c] = frc[slot, c] * r

    f, g = fa, fb
    stores = []
    for step in range(STEPS):
        field, new = fields[step], fields[step + 1]
        if step == 0:
            def before(x):
                return q0[x]
        else:
            def before(x):
                return p0[x + 1, pl.ds(8, ny), :]
            send_halo(2, field)
            prepare_faces(field)
        take_halo(2 * step, field)
        send_faces(2 * step, field)
        coarse_update(new, field, before)
        send_halo(2 * step + 1, new)
        take_faces(2 * step)
        make_ghosts(f, step, 0.0)
        fine_update(f, g, 0)
        prepare_faces(new)
        take_halo(2 * step + 1, new)
        send_faces(2 * step + 1, new)
        fine_update(f, g, 1)
        f, g = g, f
        take_faces(2 * step + 1)
        for sub in (1, 2):
            make_ghosts(f, step, sub / 3.0)
            for slot in range(2):
                fine_update(f, g, slot)
            f, g = g, f
        restrict(f, step)
        if step == STEPS - 1:
            for k, (src, dst) in enumerate([(f, fnext_h), (g, flast_h)]):
                for c in range(COLS):
                    store = pltpu.make_async_copy(
                        src.at[:, c + 1, pl.ds(8, FINE), :],
                        dst.at[:, :, pl.ds(128 * c, 128)],
                        store_sem.at[2 + k * COLS + c],
                    )
                    store.start()
                    stores.append(store)
        insert(new, step)
        out = next_h if step == STEPS - 1 else last_h
        store = pltpu.make_async_copy(new.at[mid], out, store_sem.at[step])
        if step == STEPS - 1:
            store.start()
            stores.append(store)
        else:
            last_store = store
            last_store.start()

    for phase in range(4):
        for side in range(4):
            @pl.when(exists[side])
            def _(phase=phase, side=side):
                halo_copy(phase, side).wait_send()
        for j in range(1, 4):
            face_copy(phase, j).wait_send()
    for step in range(STEPS):
        for j in range(1, 4):
            rest_copy(step, j).wait_send()
    last_store.wait()
    for store in stores:
        store.wait()


def hand_over(*refs):
    sources, targets, held, sems = refs[:4], refs[4:8], refs[8:12], refs[12]
    loads, stores = [], []
    for src, dst, mid in zip(sources, targets, held):
        parts = 4 if src.shape[0] == 64 else 2
        rows = src.shape[0] // parts
        for k in range(parts):
            at = pl.ds(k * rows, rows)
            loads.append(pltpu.make_async_copy(src.at[at], mid.at[at], sems.at[0, len(loads)]))
            stores.append(pltpu.make_async_copy(mid.at[at], dst.at[at], sems.at[1, len(stores)]))
    for load in loads:
        load.start()
    for load, store in zip(loads, stores):
        load.wait()
        store.start()
    for store in stores:
        store.wait()


def on_device(nt, nb, *args):
    coarse, fine = args[:4], args[4:8]
    anchor, inter = args[8], args[9]
    consts = [jnp.asarray(c) for c in constants()]
    f32 = jnp.float32
    smem = pl.BlockSpec(memory_space=pltpu.SMEM)
    vmem = pl.BlockSpec(memory_space=pltpu.VMEM)
    hbm = pl.BlockSpec(memory_space=pl.ANY)
    shape_c, shape_f = coarse[0].shape, fine[0].shape
    dma = pltpu.SemaphoreType.DMA
    outs = pl.pallas_call(
        functools.partial(kernel, nt, nb),
        out_shape=[jax.ShapeDtypeStruct(s, f32) for s in (shape_c, shape_c, shape_f, shape_f)],
        in_specs=[smem, smem] + [hbm] * 8 + [vmem] * len(consts),
        out_specs=[hbm] * 4,
        scratch_shapes=[
            pltpu.VMEM((66, 80, 128), f32),
            pltpu.VMEM((66, 80, 128), f32),
            pltpu.VMEM((66, 80, 128), f32),
            pltpu.VMEM((64, 64, 128), f32),
            pltpu.VMEM((64, 64, 128), f32),
            pltpu.VMEM((64, 64, 128), f32),
            pltpu.VMEM((2, COLS + 2, 64, 128), f32),
            pltpu.VMEM((2, COLS + 2, 64, 128), f32),
            pltpu.VMEM((2, COLS, FINE, 128), f32),
            pltpu.VMEM((2, COLS, FINE, 128), f32),
            pltpu.VMEM((4, 4, 64, 128), f32),
            pltpu.VMEM((4, 4, 64, 128), f32),
            pltpu.VMEM((4, 3, 2, 48, 128), f32),
            pltpu.VMEM((4, 4, 2, 48, 128), f32),
            pltpu.VMEM((2, 2, 16, 256), f32),
            pltpu.VMEM((2, 4, 2, 16, 256), f32),
            pltpu.VMEM((COLS, 96, 128), f32),
            pltpu.VMEM((4, 256, 128), f32),
            pltpu.VMEM((4, 256, 128), f32),
            pltpu.VMEM((4, 64, 128), f32),
            pltpu.VMEM((4, 256, 128), bf16),
            pltpu.VMEM((4, 256, 128), bf16),
            dma((4, 4)), dma((4, 4)), dma((4, 3)), dma((4, 3)), dma((2, 3)), dma((2, 3)),
            dma((4 + 4 * COLS,)), dma((2 + 2 * COLS,)),
        ],
        compiler_params=pltpu.CompilerParams(
            collective_id=0, has_side_effects=True, vmem_limit_bytes=56 * 1024 * 1024
        ),
        cost_estimate=pl.CostEstimate(flops=40_000_000, bytes_accessed=20_000_000, transcendentals=0),
        name="wave",
    )(inter, anchor, *coarse, *fine, *consts)
    return pl.pallas_call(
        hand_over,
        out_shape=[jax.ShapeDtypeStruct(o.shape, f32) for o in outs],
        in_specs=[hbm] * 4,
        out_specs=[hbm] * 4,
        scratch_shapes=[pltpu.VMEM(o.shape, f32) for o in outs] + [dma((2, 12))],
        compiler_params=pltpu.CompilerParams(vmem_limit_bytes=32 * 1024 * 1024),
        name="hand_over",
    )(*outs)


def solution(mesh):
    whole = ("tile", "bulk")
    c, f = P("tile", "bulk", None), P(whole, None, None)
    return jax.shard_map(
        functools.partial(on_device, mesh.shape["tile"], mesh.shape["bulk"]),
        mesh=mesh,
        in_specs=(c, c, c, c, f, f, f, f, P(whole, None), f),
        out_specs=(c, c, f, f),
        check_vma=False,
    )
```

```python
import functools

import jax
import jax.numpy as jnp
import ml_dtypes
import numpy as np
from jax import lax
from jax.experimental import pallas as pl
from jax.experimental.pallas import tpu as pltpu
from jax.sharding import PartitionSpec as P

STEPS = 2
MESH = pl.DeviceIdType.MESH
BC, FINE = 16, 48
ROW = FINE * FINE
COLS = ROW // 128
bf16 = jnp.bfloat16


def constants():
    flat = np.arange(ROW)
    y, z = flat // FINE, flat % FINE
    group = np.arange(BC)[:, None]
    spread = np.zeros((128, ROW), np.float32)
    spread[0:16] = (y == 0) & (z // 3 == group)
    spread[16:32] = (y == FINE - 1) & (z // 3 == group)
    spread[32:48] = (z == 0) & (y // 3 == group)
    spread[48:64] = (z == FINE - 1) & (y // 3 == group)
    spread[64:80] = z // 3 == group
    spread = np.concatenate([spread, spread], 0)
    up = np.zeros((160, 96), np.float32)
    for box in range(2):
        for x in range(FINE):
            up[box * 48 + x, box * 48 + x // 3] = 1
        for r in range(32):
            up[96 + box * 32 + r, box * 48 + 16 + r] = 1
    rows = (y // 3 == group).astype(np.float32)
    rows = rows.reshape(BC, COLS, 128).transpose(1, 0, 2)
    inside = np.stack([np.tile(z != 0, (8, 1)), np.tile(z != FINE - 1, (8, 1))]).astype(np.float32)
    inside = inside.reshape(2, 8, COLS, 128)[:, :, :3].transpose(2, 0, 1, 3)
    down = np.zeros((16, 96), np.float32)
    for x in range(FINE):
        down[x // 3, x] = 1
        down[x // 3, 48 + x] = 1
    gather = np.zeros((ROW, 256), np.float32)
    gather[flat, (y // 3) * 16 + z // 3] = 1
    rep = np.zeros((256, 16), np.float32)
    rep[np.arange(256), np.arange(256) // 16] = 1
    own = (np.arange(256)[:, None] % 16 == np.arange(256)[None] // 16).astype(np.float32)
    tile = (np.arange(256)[:, None] % 16 == np.arange(128)[None] % 16).astype(np.float32)
    tile = np.concatenate([tile, tile], 0)
    half = ml_dtypes.bfloat16
    return [
        spread.astype(half), up.astype(half), rows, inside, down.astype(half),
        gather.astype(half), rep.astype(half), own, tile.astype(half),
    ]


def split(value):
    high = value.astype(bf16)
    low = (value - high.astype(jnp.float32)).astype(bf16)
    return high, low


def dot(a, b):
    return jnp.dot(a, b, preferred_element_type=jnp.float32)


def kernel(
    nt, nb,
    inter, anchor,
    now_h, before_h, courant_h, absorb_h, fnow_h, fbefore_h, fcourant_h, fabsorb_h,
    spread, up, rows, inside, down, gather, rep, own, tile,
    next_h, last_h, fnext_h, flast_h,
    p0, p1, p2, q0, rc, r2, fa, fb, frc, fr2,
    halo_out, halo_in, face_out, face_in, rest_out, rest_in,
    ghost, blocks, cubes, edges, picks, windows,
    halo_ss, halo_rs, face_ss, face_rs, rest_ss, rest_rs, load_sem, store_sem,
):
    t, b = lax.axis_index("tile"), lax.axis_index("bulk")
    fields = [p0, p1, p2]
    nx, ny = 64, 64

    exists = [t > 0, t < nt - 1, b > 0, b < nb - 1]
    missing = [t == 0, t == nt - 1, b == 0, b == nb - 1]
    beside = [(t - 1, b), (t + 1, b), (t, b - 1), (t, b + 1)]
    b_other = b + 1 - 2 * lax.rem(b, 2)
    t_other = lax.rem(t + nt // 2, nt)
    quad = [(t, b), (t, b_other), (t_other, b), (t_other, b_other)]

    mid = (pl.ds(1, nx), pl.ds(8, ny), slice(None))
    loads = [
        pltpu.make_async_copy(src, dst, load_sem.at[i])
        for i, (src, dst) in enumerate([
            (now_h, p0.at[mid]),
            (before_h, q0),
            (courant_h, rc),
            (absorb_h, r2),
        ] + [
            (src.at[:, :, pl.ds(128 * c, 128)], dst)
            for c in range(COLS)
            for src, dst in (
                (fcourant_h, frc.at[:, c]),
                (fabsorb_h, fr2.at[:, c]),
                (fnow_h, fa.at[:, c + 1, pl.ds(8, FINE), :]),
                (fbefore_h, fb.at[:, c + 1, pl.ds(8, FINE), :]),
            )
        ])
    ]
    for load in loads:
        load.start()

    barrier = pltpu.get_barrier_semaphore()
    for have, device in zip(exists, beside):
        @pl.when(have)
        def _(device=device):
            pl.semaphore_signal(barrier, inc=1, device_id=device, device_id_type=MESH)
    for device in quad[2:]:
        pl.semaphore_signal(barrier, inc=1, device_id=device, device_id_type=MESH)
    peers = jnp.int32(2)
    for have in exists:
        peers = peers + jnp.where(have, 1, 0)

    zero_side = jnp.zeros((2, 64, 128), jnp.float32)
    for buf in (fa, fb):
        buf[:, 0] = zero_side
        buf[:, COLS + 1] = zero_side

    lane = lax.broadcasted_iota(jnp.int32, (64, 128), 1)
    not_first, not_last = lane != 0, lane != 127

    def halo_wait(phase, side):
        return pltpu.make_async_remote_copy(
            src_ref=halo_out.at[phase, side],
            dst_ref=halo_in.at[phase, side],
            send_sem=halo_ss.at[phase, side],
            recv_sem=halo_rs.at[phase, side],
            device_id=beside[side],
            device_id_type=MESH,
        )

    def halo_copy(phase, side):
        return pltpu.make_async_remote_copy(
            src_ref=halo_out.at[phase, side],
            dst_ref=halo_in.at[phase, side ^ 1],
            send_sem=halo_ss.at[phase, side],
            recv_sem=halo_rs.at[phase, side ^ 1],
            device_id=beside[side],
            device_id_type=MESH,
        )

    def send_halo(phase, field):
        halo_out[phase, 0] = field[1, pl.ds(8, ny), :]
        halo_out[phase, 1] = field[nx, pl.ds(8, ny), :]
        halo_out[phase, 2] = field[pl.ds(1, nx), 8, :]
        halo_out[phase, 3] = field[pl.ds(1, nx), 7 + ny, :]
        for side in range(4):
            @pl.when(exists[side])
            def _(side=side):
                halo_copy(phase, side).start()

    def take_halo(phase, field):
        for side in range(4):
            @pl.when(exists[side])
            def _(side=side):
                halo_wait(phase, side).wait_recv()

            @pl.when(missing[side])
            def _(side=side):
                halo_in[phase, side] = jnp.zeros((64, 128), jnp.float32)
        field[0, pl.ds(8, ny), :] = halo_in[phase, 0]
        field[nx + 1, pl.ds(8, ny), :] = halo_in[phase, 1]
        field[pl.ds(1, nx), 7, :] = halo_in[phase, 2]
        field[pl.ds(1, nx), 8 + ny, :] = halo_in[phase, 3]

    def face_copy(phase, j):
        return pltpu.make_async_remote_copy(
            src_ref=face_out.at[phase, j - 1],
            dst_ref=face_in.at[phase, j],
            send_sem=face_ss.at[phase, j - 1],
            recv_sem=face_rs.at[phase, j - 1],
            device_id=quad[j],
            device_id_type=MESH,
        )

    def rest_copy(step, j):
        return pltpu.make_async_remote_copy(
            src_ref=rest_out.at[step],
            dst_ref=rest_in.at[step, j],
            send_sem=rest_ss.at[step, j - 1],
            recv_sem=rest_rs.at[step, j - 1],
            device_id=quad[j],
            device_id_type=MESH,
        )

    lane16 = lax.broadcasted_iota(jnp.int32, (16, 128), 1)
    z_in = lax.broadcasted_iota(jnp.int32, (256, 128), 0)
    z_in = lax.rem(z_in, 128)
    z_out = lax.broadcasted_iota(jnp.int32, (256, 128), 1)
    y_row = lax.broadcasted_iota(jnp.int32, (16, 16, 128), 1)
    y_lane = lax.rem(lax.broadcasted_iota(jnp.int32, (16, 16, 128), 2), 16)

    at = [4 * lax.div(inter[0, 1, e], 16) + lax.div(inter[0, 2, e], 16) for e in range(4)]
    spots = [jnp.full((16, 128), a, jnp.int32) for a in at]

    def choose(load, height, store):
        values = [None] * 4
        for i in range(4):
            for j in range(4):
                value = load(i, j)
                for e in range(4):
                    if i + j == 0:
                        values[e] = value
                    else:
                        values[e] = jnp.where(spots[e][:height] == 4 * i + j, value, values[e])
        for e in range(4):
            store(e, values[e])

    def collect(field):
        def to_edges(row, height):
            def store(e, value):
                edges[e, pl.ds(row, height), :] = value
            return store

        choose(lambda i, j: field[16 * i, pl.ds(8 + 16 * j, 16), :], 16, to_edges(32, 16))
        choose(lambda i, j: field[16 * i + 17, pl.ds(8 + 16 * j, 16), :], 16, to_edges(48, 16))

        choose(lambda i, j: field[pl.ds(16 * i + 1, 16), 7 + 16 * j, :], 16, to_edges(0, 16))
        choose(lambda i, j: field[pl.ds(16 * i + 1, 16), 24 + 16 * j, :], 16, to_edges(16, 16))

    def prepare_faces(field):
        @pl.loop(0, 16, unroll=4)
        def _(u):
            def to_cubes(e, value):
                cubes[e, pl.ds(pl.multiple_of(16 * u, 16), 16), :] = value
            choose(lambda i, j: field[16 * i + 1 + u, pl.ds(8 + 16 * j, 16), :], 16, to_cubes)

        @pl.loop(0, 4, unroll=4)
        def _(entry):
            high, low = split(cubes[entry])
            zs = dot(jnp.concatenate([high, low], axis=1), picks[entry]).reshape(16, 16, 128)
            blocks[entry, pl.ds(0, 16), :] = jnp.sum(jnp.where(y_row == y_lane, zs, 0.0), axis=1)

    def make_picks():
        @pl.loop(0, 4, unroll=4)
        def _(entry):
            z0 = inter[0, 3, entry]
            pick = ((z_in == z0 - 1) & (z_out >= 32) & (z_out < 48)) | (
                (z_in == z0 + 16) & (z_out >= 48) & (z_out < 64)
            )
            picks[entry] = jnp.where(pick, 1.0, 0.0).astype(bf16)
            windows[entry] = jnp.where(z_in == z0 + lax.rem(z_out, 16), 1.0, 0.0).astype(bf16)

    def faces_of(ref, entry):
        high, low = split(edges[entry])
        flat = dot(jnp.concatenate([high, low], axis=1), windows[entry])
        zs = ref[pl.ds(0, 16), :]
        first = jnp.where(lane16 < 16, flat[0:16], jnp.where(lane16 < 32, flat[16:32], zs))
        x_lanes = (lane16 >= 64) & (lane16 < 80)
        ref[pl.ds(0, 16), :] = jnp.where(lane16 < 64, first, 0.0)
        ref[pl.ds(16, 16), :] = jnp.where(x_lanes, flat[32:48], 0.0)
        ref[pl.ds(32, 16), :] = jnp.where(x_lanes, flat[48:64], 0.0)

    def faces_for(j, slot):
        target = 2 * (quad[j][0] * nb + quad[j][1]) + slot
        value = blocks[0, pl.ds(0, 48), :]
        for entry in range(1, 4):
            hit = inter[0, 0, entry] == target
            value = jnp.where(hit, blocks[entry, pl.ds(0, 48), :], value)
        return value

    def send_faces(phase, field):
        collect(field)

        @pl.loop(0, 4, unroll=4)
        def _(entry):
            faces_of(blocks.at[entry, pl.ds(0, 48), :], entry)
        for j in range(1, 4):
            for slot in range(2):
                face_out[phase, j - 1, slot] = faces_for(j, slot)
            face_copy(phase, j).start()
        for slot in range(2):
            face_in[phase, 0, slot] = faces_for(0, slot)

    def take_faces(phase):
        for j in range(1, 4):
            face_copy(phase, j).wait_recv()

    def source_of(slot):
        away_t = jnp.where(lax.div(anchor[slot, 0], 64) == t, 0, 2)
        away_b = jnp.where(lax.div(anchor[slot, 1], 64) == b, 0, 1)
        return away_t + away_b

    sources = [source_of(slot) for slot in range(2)]

    def arrived(phase, slot):
        value = face_in[phase, 0, slot]
        for j in range(1, 4):
            value = jnp.where(sources[slot] == j, face_in[phase, j, slot], value)
        return value

    def coarse_update(new, field, before):
        @pl.loop(0, nx, unroll=8)
        def _(x):
            c = field[x + 1, pl.ds(8, ny), :]
            nbs = field[x, pl.ds(8, ny), :] + field[x + 2, pl.ds(8, ny), :]
            nbs = nbs + field[x + 1, pl.ds(7, ny), :] + field[x + 1, pl.ds(9, ny), :]
            nbs = nbs + jnp.where(not_first, pltpu.roll(c, 1, 1), 0.0)
            nbs = nbs + jnp.where(not_last, pltpu.roll(c, 127, 1), 0.0)
            old = before(x)
            new[x + 1, pl.ds(8, ny), :] = old + r2[x] * (c - old) + rc[x] * (nbs - 6.0 * c)

    def make_ghosts(f, phase, weight):
        parts = []
        for slot in range(2):
            q = arrived(2 * phase, slot)
            if weight:
                q = q + weight * (arrived(2 * phase + 1, slot) - q)
            parts.append(q)
        high, low = split(jnp.concatenate(parts, axis=0))
        left = dot(up[...], jnp.concatenate([high, low], axis=1)).astype(bf16)

        @pl.loop(0, 9, unroll=9)
        def _(c):
            both = dot(left, spread[:, pl.ds(pl.multiple_of(c * 256, 256), 256)])
            for half in range(2):
                col = 2 * c + half
                part = both[:, 128 * half:128 * half + 128]
                ghost[col] = part[:96]
                for slot in range(2):
                    for k in range(2):
                        first = 96 + 32 * slot + 16 * k
                        face = part[first:first + 16] * rows[col]
                        f[slot, col + 1, pl.ds(7 + 49 * k, 1), :] = jnp.sum(face, axis=0, keepdims=True)

    lane8 = lax.broadcasted_iota(jnp.int32, (8, 128), 1)
    under = {shift: lane8 < shift for shift in (1, 48, 80, 127)}

    def fine_update(f, g, slot):
        @pl.loop(0, 6, unroll=3)
        def _(i):
            base = pl.multiple_of(8 * i, 8)

            def turned(col):
                value = f[slot, col, pl.ds(pl.multiple_of(base + 8, 8), 8), :]
                return value, {shift: pltpu.roll(value, shift, 1) for shift in under}

            _, before = turned(0)
            c, here = turned(1)
            for col in range(COLS):
                later, after = turned(col + 2)
                nbs = f[slot, col + 1, pl.ds(base + 7, 8), :] + f[slot, col + 1, pl.ds(base + 9, 8), :]
                nbs = nbs + jnp.where(under[48], before[48], here[48])
                nbs = nbs + jnp.where(under[80], here[80], after[80])
                nbs = nbs + jnp.where(under[1], before[1], here[1]) * inside[col % 3, 0]
                nbs = nbs + jnp.where(under[127], here[127], after[127]) * inside[col % 3, 1]
                nbs = nbs + ghost[col, pl.ds(pl.multiple_of(48 * slot + base, 8), 8), :]
                place = (slot, col + 1, pl.ds(pl.multiple_of(base + 8, 8), 8), slice(None))
                old = g[place]
                coef = (slot, col, pl.ds(base, 8), slice(None))
                g[place] = old + fr2[coef] * (c - old) + frc[coef] * (nbs - 6.0 * c)
                before, here, c = here, after, later

    def restrict(f, step):
        means = jnp.zeros((64, 256), jnp.float32)
        for pair in range(COLS // 2):
            lefts = []
            for slot in range(2):
                cols = [f[slot, 2 * pair + 1 + k, pl.ds(8, FINE), :] for k in range(2)]
                high, low = split(jnp.concatenate(cols, axis=1))
                lefts.extend(split(dot(down[...], jnp.concatenate([high, low], axis=0))))
            means = means + dot(jnp.concatenate(lefts, axis=0), gather[pl.ds(256 * pair, 256), :])
        for slot in range(2):
            mean = (means[32 * slot:32 * slot + 16] + means[32 * slot + 16:32 * slot + 32]) * (1.0 / 27.0)
            rest_out[step, slot] = mean
            rest_in[step, 0, slot] = mean
        for j in range(1, 4):
            rest_copy(step, j).start()

    def insert(new, step):
        for j in range(1, 4):
            rest_copy(step, j).wait_recv()

        @pl.loop(0, 4, unroll=4)
        def _(entry):
            value = rest_in[step, 0, 0]
            for j in range(4):
                for slot in range(2):
                    hit = inter[0, 0, entry] == 2 * (quad[j][0] * nb + quad[j][1]) + slot
                    value = jnp.where(hit, rest_in[step, j, slot], value)
            high, low = split(value)
            left = [(dot(rep[...], part) * own[...]).astype(bf16) for part in (high, low)]
            blocks[entry] = dot(jnp.concatenate(left, axis=1), tile[...])

        place = lax.div(lane16, 16)

        @pl.loop(0, 4)
        def _(i):
            for j in range(4):
                masks = []
                for entry in range(4):
                    hit = (inter[0, 0, entry] >= 0) & (inter[0, 1, entry] == 16 * i) & (inter[0, 2, entry] == 16 * j)
                    at = jnp.where(hit, lax.div(inter[0, 3, entry], 16), -1)
                    masks.append(place == at)

                @pl.loop(0, 16, unroll=16)
                def _(x):
                    where = (16 * i + x + 1, pl.ds(8 + 16 * j, 16), slice(None))
                    value = new[where]
                    for entry in range(4):
                        block = blocks[entry, pl.ds(pl.multiple_of(16 * x, 16), 16), :]
                        value = jnp.where(masks[entry], block, value)
                    new[where] = value

    make_picks()
    loads[0].wait()
    pl.semaphore_wait(barrier, peers)
    send_halo(0, p0)
    prepare_faces(p0)
    for load in loads[1:4]:
        load.wait()

    @pl.loop(0, nx, unroll=8)
    def _(x):
        r = 1.0 / (1.0 + r2[x])
        r2[x] = 2.0 * r
        rc[x] = rc[x] * r

    for load in loads[4:]:
        load.wait()

    for slot in range(2):
        @pl.loop(0, COLS, unroll=6)
        def _(c):
            r = 1.0 / (1.0 + fr2[slot, c])
            fr2[slot, c] = 2.0 * r
            frc[slot, c] = frc[slot, c] * r

    f, g = fa, fb
    stores = []
    for step in range(STEPS):
        field, new = fields[step], fields[step + 1]
        if step == 0:
            def before(x):
                return q0[x]
        else:
            def before(x):
                return p0[x + 1, pl.ds(8, ny), :]
            send_halo(2, field)
            prepare_faces(field)
        take_halo(2 * step, field)
        send_faces(2 * step, field)
        coarse_update(new, field, before)
        send_halo(2 * step + 1, new)
        take_faces(2 * step)
        make_ghosts(f, step, 0.0)
        fine_update(f, g, 0)
        prepare_faces(new)
        take_halo(2 * step + 1, new)
        send_faces(2 * step + 1, new)
        fine_update(f, g, 1)
        f, g = g, f
        take_faces(2 * step + 1)
        for sub in (1, 2):
            make_ghosts(f, step, sub / 3.0)
            for slot in range(2):
                fine_update(f, g, slot)
            f, g = g, f
        restrict(f, step)
        if step == STEPS - 1:
            for k, (src, dst) in enumerate([(f, fnext_h), (g, flast_h)]):
                for c in range(COLS):
                    store = pltpu.make_async_copy(
                        src.at[:, c + 1, pl.ds(8, FINE), :],
                        dst.at[:, :, pl.ds(128 * c, 128)],
                        store_sem.at[2 + k * COLS + c],
                    )
                    store.start()
                    stores.append(store)
        insert(new, step)
        out = next_h if step == STEPS - 1 else last_h
        store = pltpu.make_async_copy(new.at[mid], out, store_sem.at[step])
        if step == STEPS - 1:
            store.start()
            stores.append(store)
        else:
            last_store = store
            last_store.start()

    for phase in range(4):
        for side in range(4):
            @pl.when(exists[side])
            def _(phase=phase, side=side):
                halo_copy(phase, side).wait_send()
        for j in range(1, 4):
            face_copy(phase, j).wait_send()
    for step in range(STEPS):
        for j in range(1, 4):
            rest_copy(step, j).wait_send()
    last_store.wait()
    for store in stores:
        store.wait()


def hand_over(*refs):
    sources, targets, held, sems = refs[:4], refs[4:8], refs[8:12], refs[12]
    loads, stores = [], []
    for src, dst, mid in zip(sources, targets, held):
        parts = 4 if src.shape[0] == 64 else 2
        rows = src.shape[0] // parts
        for k in range(parts):
            at = pl.ds(k * rows, rows)
            loads.append(pltpu.make_async_copy(src.at[at], mid.at[at], sems.at[0, len(loads)]))
            stores.append(pltpu.make_async_copy(mid.at[at], dst.at[at], sems.at[1, len(stores)]))
    for load in loads:
        load.start()
    for load, store in zip(loads, stores):
        load.wait()
        store.start()
    for store in stores:
        store.wait()


def on_device(nt, nb, *args):
    coarse, fine = args[:4], args[4:8]
    anchor, inter = args[8], args[9]
    consts = [jnp.asarray(c) for c in constants()]
    f32 = jnp.float32
    smem = pl.BlockSpec(memory_space=pltpu.SMEM)
    vmem = pl.BlockSpec(memory_space=pltpu.VMEM)
    hbm = pl.BlockSpec(memory_space=pl.ANY)
    shape_c, shape_f = coarse[0].shape, fine[0].shape
    dma = pltpu.SemaphoreType.DMA
    outs = pl.pallas_call(
        functools.partial(kernel, nt, nb),
        out_shape=[jax.ShapeDtypeStruct(s, f32) for s in (shape_c, shape_c, shape_f, shape_f)],
        in_specs=[smem, smem] + [hbm] * 8 + [vmem] * len(consts),
        out_specs=[hbm] * 4,
        scratch_shapes=[
            pltpu.VMEM((66, 80, 128), f32),
            pltpu.VMEM((66, 80, 128), f32),
            pltpu.VMEM((66, 80, 128), f32),
            pltpu.VMEM((64, 64, 128), f32),
            pltpu.VMEM((64, 64, 128), f32),
            pltpu.VMEM((64, 64, 128), f32),
            pltpu.VMEM((2, COLS + 2, 64, 128), f32),
            pltpu.VMEM((2, COLS + 2, 64, 128), f32),
            pltpu.VMEM((2, COLS, FINE, 128), f32),
            pltpu.VMEM((2, COLS, FINE, 128), f32),
            pltpu.VMEM((4, 4, 64, 128), f32),
            pltpu.VMEM((4, 4, 64, 128), f32),
            pltpu.VMEM((4, 3, 2, 48, 128), f32),
            pltpu.VMEM((4, 4, 2, 48, 128), f32),
            pltpu.VMEM((2, 2, 16, 256), f32),
            pltpu.VMEM((2, 4, 2, 16, 256), f32),
            pltpu.VMEM((COLS, 96, 128), f32),
            pltpu.VMEM((4, 256, 128), f32),
            pltpu.VMEM((4, 256, 128), f32),
            pltpu.VMEM((4, 64, 128), f32),
            pltpu.VMEM((4, 256, 128), bf16),
            pltpu.VMEM((4, 256, 128), bf16),
            dma((4, 4)), dma((4, 4)), dma((4, 3)), dma((4, 3)), dma((2, 3)), dma((2, 3)),
            dma((4 + 4 * COLS,)), dma((2 + 2 * COLS,)),
        ],
        compiler_params=pltpu.CompilerParams(
            collective_id=0, has_side_effects=True, vmem_limit_bytes=56 * 1024 * 1024
        ),
        cost_estimate=pl.CostEstimate(flops=40_000_000, bytes_accessed=20_000_000, transcendentals=0),
        name="wave",
    )(inter, anchor, *coarse, *fine, *consts)
    return pl.pallas_call(
        hand_over,
        out_shape=[jax.ShapeDtypeStruct(o.shape, f32) for o in outs],
        in_specs=[hbm] * 4,
        out_specs=[hbm] * 4,
        scratch_shapes=[pltpu.VMEM(o.shape, f32) for o in outs] + [dma((2, 12))],
        compiler_params=pltpu.CompilerParams(vmem_limit_bytes=60 * 1024 * 1024),
        name="hand_over",
    )(*outs)


def solution(mesh):
    whole = ("tile", "bulk")
    c, f = P("tile", "bulk", None), P(whole, None, None)
    return jax.shard_map(
        functools.partial(on_device, mesh.shape["tile"], mesh.shape["bulk"]),
        mesh=mesh,
        in_specs=(c, c, c, c, f, f, f, f, P(whole, None), f),
        out_specs=(c, c, f, f),
        check_vma=False,
    )
```
